32 devices in a mesh: seq: 8 (over z, x), tp: 4 (over y, core).
Axes of the slice: x: 2, y: 2, z: 4, core: 2. Of those that a mesh axis runs over, the one named last changes fastest.
Arguments:
- layer_input: bfloat16 [2048, 2048], P('seq'), may hold values from -1.5 to 1.5
- norm_gain: float32 [2048], replicated, may hold values from 0.5 to 1.5
- w_query: bfloat16 [2048, 2048], P(None, 'tp')
- key_weight: bfloat16 [2048, 1024], P(None, 'tp')
- value_weight: bfloat16 [2048, 1024], P(None, 'tp'), may hold values from -0.125 to 0.125
- w_out: bfloat16 [2048, 2048], P('tp'), may hold values from -1 to 1
- query_gain: float32 [128], replicated, may hold values from 0.6 to 6, as said below
- key_gain: float32 [128], replicated, may hold values from 0.6 to 6, as said below
- seg_ids: int32 [2048], P('seq'), may hold values from 0 to 7, as said below
- positions: int32 [2048], P('seq'), may hold values from 0 to 1637, as said below
- post_gain: float32 [2048], replicated, may hold values from 0.5 to 1.5
- w_gate: bfloat16 [2048, 3072], P('seq', 'tp'), may hold values from -0.125 to 0.125
- w_up: bfloat16 [2048, 3072], P('seq', 'tp'), may hold values from -0.125 to 0.125
- w_down: bfloat16 [3072, 2048], P('tp', 'seq'), may hold values from -0.21875 to 0.21875
Outputs:
- hidden: bfloat16 [2048, 2048], P('seq')
- key_cache: bfloat16 [2048, 1024], P('seq', 'tp')
- value_cache: bfloat16 [2048, 1024], P('seq', 'tp')
The draws below stay inside these ranges and needn't reach their ends.
Inputs may be any that keep to these rules, and one draw needn't show every extreme that they name: `seg_ids`: prompt numbers never fall along the stream; each of the 8 prompts is a contiguous run of one or more tokens, and one prompt has exactly 1638 tokens. `positions`: each token's place in its prompt, counting from 0 at the prompt's first token. `query_gain`: positive gains. `key_gain`: positive gains.
All inputs are finite; a program needn't handle non-finite values.
Results may differ from the reference program's by a relative error of at most 0.02.
Values may be sent and summed in bfloat16 or wider, within the bound.
No kernel may reach another device: no remote copies, remote signals or barrier semaphores. Data moves between devices by JAX's collectives and lax.ppermute only.
A program may use at most 128 MiB of HBM per device.

```python
import math
import jax
import jax.numpy as jnp
from jax import lax

MODEL_WIDTH = 2048
QUERY_HEADS = 16
KEY_VALUE_HEADS = 8
HEAD_DIM = 128
FF = 3072
SEGS = 8
PACKED_TOKENS = 2048
LEN_MAX = 1638


def tied_pair(key):
    query_slice = jax.random.normal(jax.random.fold_in(key, 101), (MODEL_WIDTH, QUERY_HEADS * HEAD_DIM), jnp.float32) / math.sqrt(MODEL_WIDTH)
    key_slice = jax.random.normal(jax.random.fold_in(key, 102), (MODEL_WIDTH, KEY_VALUE_HEADS * HEAD_DIM), jnp.float32) / math.sqrt(MODEL_WIDTH)
    return (query_slice, key_slice)


def draw_w_query(key, part):
    return tied_pair(key)[0].astype(jnp.bfloat16)


def draw_key_weight(key, part):
    return tied_pair(key)[1].astype(jnp.bfloat16)


def head_gains(key, salt):
    picked = jax.random.uniform(jax.random.fold_in(key, salt), (HEAD_DIM,), jnp.float32)
    return 0.6 + 0.8 * picked


def draw_query_gain(key, part):
    return head_gains(key, 201)


def draw_key_gain(key, part):
    return head_gains(key, 202)


def layout(key):
    longest = jax.random.randint(jax.random.fold_in(key, 11), (), 0, SEGS)
    index = jnp.arange(SEGS, dtype=jnp.int32)
    weights = jax.random.randint(jax.random.fold_in(key, 12), (SEGS,), 1, 101)
    weights = jnp.where(index == longest, 0, weights)
    extra = PACKED_TOKENS - LEN_MAX - (SEGS - 1)
    share = extra * weights // jnp.sum(weights)
    leftover = extra - jnp.sum(share)
    first_other = jnp.where(longest == 0, 1, 0)
    share = share + jnp.where(index == first_other, leftover, 0)
    lengths = jnp.where(index == longest, LEN_MAX, 1 + share).astype(jnp.int32)
    ends = jnp.cumsum(lengths)
    starts = ends - lengths
    place = jnp.arange(PACKED_TOKENS, dtype=jnp.int32)
    segment = jnp.sum((place[:, None] >= ends[None, :]).astype(jnp.int32), axis=1)
    onehot = (segment[:, None] == index[None, :]).astype(jnp.int32)
    offset = place - jnp.sum(onehot * starts[None, :], axis=1)
    return (segment.astype(jnp.int32), offset.astype(jnp.int32))


def draw_seg_ids(key, part):
    return layout(key)[0]


def draw_positions(key, part):
    return layout(key)[1]


def levels(own_key, dims, cuts, least, high):
    def one(position, shards_of):
        heights = jax.random.uniform(jax.random.fold_in(jax.random.fold_in(own_key, 6), position), (shards_of,), jnp.float32, least / len(cuts), high / len(cuts))
        return jnp.repeat(jnp.exp(heights), dims[position] // shards_of).reshape((-1,) + (1,) * (len(dims) - position - 1))

    loudness = one(*cuts[0])
    for cut in cuts[1:]:
        loudness = loudness * one(*cut)
    return loudness


def normal_values(own_key, dims, deviation, most, cuts=(), kind=jnp.bfloat16):
    entries = jax.random.normal(own_key, dims, jnp.float32) * deviation
    if len(cuts) > 0:
        entries = levels(own_key, dims, cuts, -0.22, 0.18) * entries
    return jnp.clip(entries, min=-most, max=most).astype(kind)


def setup_inputs(seed: int = 0) -> dict:
    splits = jax.random.split(jax.random.key(seed), 15)
    return {
        "layer_input": normal_values(splits[0], (PACKED_TOKENS, MODEL_WIDTH), 0.25, 1.5, ((0, 8),)),
        "norm_gain": jnp.clip(1.0 + 0.1 * jax.random.normal(splits[1], (MODEL_WIDTH,), jnp.float32), 0.5, 1.5),
        "w_query": draw_w_query(jax.random.fold_in(splits[14], 71), 0),
        "key_weight": draw_key_weight(jax.random.fold_in(splits[14], 71), 0),
        "value_weight": normal_values(splits[4], (MODEL_WIDTH, KEY_VALUE_HEADS * HEAD_DIM), MODEL_WIDTH ** -0.5, 0.125, ((1, 4),)),
        "w_out": normal_values(splits[5], (QUERY_HEADS * HEAD_DIM, MODEL_WIDTH), (HEAD_DIM // 4) ** -0.5, 1.0, ((0, 4),)),
        "query_gain": draw_query_gain(jax.random.fold_in(splits[14], 71), 0),
        "key_gain": draw_key_gain(jax.random.fold_in(splits[14], 71), 0),
        "seg_ids": draw_seg_ids(jax.random.fold_in(splits[14], 71), 0),
        "positions": draw_positions(jax.random.fold_in(splits[14], 71), 0),
        "post_gain": jnp.clip(1.0 + 0.1 * jax.random.normal(splits[10], (MODEL_WIDTH,), jnp.float32), 0.5, 1.5),
        "w_gate": normal_values(splits[11], (MODEL_WIDTH, FF), MODEL_WIDTH ** -0.5, 0.125, ((0, 8), (1, 4))),
        "w_up": normal_values(splits[12], (MODEL_WIDTH, FF), MODEL_WIDTH ** -0.5, 0.125, ((0, 8), (1, 4))),
        "w_down": normal_values(splits[13], (FF, MODEL_WIDTH), (FF // 4) ** -0.5, 0.21875, ((0, 4), (1, 8))),
    }


def rms(v, gain):
    return v * lax.rsqrt(lax.optimization_barrier(jnp.mean(v * v, axis=-1, keepdims=True)) + 1e-06) * gain

def rope(v, place):
    half = v.shape[-1] // 2
    freqs = 1000000.0 ** (-2.0 * jnp.arange(half, dtype=jnp.float32) / v.shape[-1])
    angle = place.astype(jnp.float32)[:, None] * freqs[None, :]
    cosine = jnp.cos(angle)[:, None, :]
    sine = jnp.sin(angle)[:, None, :]
    block_start = v[..., :half]
    second = v[..., half:]
    return jnp.concatenate([block_start * cosine - second * sine, second * cosine + block_start * sine], axis=-1)

def reference(layer_input, norm_gain, w_query, key_weight, value_weight, w_out, query_gain, key_gain, seg_ids, positions, post_gain, w_gate, w_up, w_down):
    xf = layer_input.astype(jnp.float32)
    normed_input = rms(xf, norm_gain).astype(jnp.bfloat16)
    query_matrix = jnp.dot(normed_input, w_query, preferred_element_type=jnp.float32).reshape(PACKED_TOKENS, QUERY_HEADS, HEAD_DIM)
    query_matrix = rope(rms(query_matrix, query_gain), positions).astype(jnp.bfloat16)
    key_matrix = jnp.dot(normed_input, key_weight, preferred_element_type=jnp.float32).reshape(PACKED_TOKENS, KEY_VALUE_HEADS, HEAD_DIM)
    key_matrix = rope(rms(key_matrix, key_gain), positions).astype(jnp.bfloat16)
    value_matrix = jnp.dot(normed_input, value_weight, preferred_element_type=jnp.float32).astype(jnp.bfloat16)
    key_heads = key_matrix.transpose(1, 0, 2)
    heads_of_value = value_matrix.reshape(PACKED_TOKENS, KEY_VALUE_HEADS, HEAD_DIM).transpose(1, 0, 2)
    head_group = QUERY_HEADS // KEY_VALUE_HEADS
    scale = 1.0 / math.sqrt(HEAD_DIM)
    token_block = math.gcd(PACKED_TOKENS, 512)
    outputs = []
    for block_start in range(0, PACKED_TOKENS, token_block):
        block_end = block_start + token_block
        block_queries = query_matrix[block_start:block_end].reshape(token_block, KEY_VALUE_HEADS, head_group, HEAD_DIM).transpose(1, 0, 2, 3)
        allowed = (seg_ids[block_start:block_end][:, None] == seg_ids[:block_end][None, :]) & (positions[:block_end][None, :] <= positions[block_start:block_end][:, None])

        def one_head(items):
            qh, kh, vh = items
            s = jnp.einsum('qgd,kd->gqk', qh.astype(jnp.float32), kh.astype(jnp.float32)) * scale
            s = jnp.where(allowed[None], s, -1e+30)
            top = lax.optimization_barrier(jnp.max(s, axis=-1, keepdims=True))
            p = jnp.where(allowed[None], jnp.exp(s - top), 0.0)
            total = lax.optimization_barrier(jnp.sum(p, axis=-1, keepdims=True))
            pb = p.astype(jnp.bfloat16).astype(jnp.float32)
            return jnp.einsum('gqk,kd->qgd', pb, vh.astype(jnp.float32)) / total.transpose(1, 0, 2)
        heads = lax.map(one_head, (block_queries, key_heads[:, :block_end], heads_of_value[:, :block_end]))
        outputs.append(heads.transpose(1, 0, 2, 3).reshape(token_block, QUERY_HEADS * HEAD_DIM))
    attended = jnp.concatenate(outputs, axis=0).astype(jnp.bfloat16)
    mid = (xf + jnp.dot(attended, w_out, preferred_element_type=jnp.float32)).astype(jnp.bfloat16)
    mid_f = mid.astype(jnp.float32)
    post_normed = rms(mid_f, post_gain).astype(jnp.bfloat16)
    gate = jnp.dot(post_normed, w_gate, preferred_element_type=jnp.float32)
    up = jnp.dot(post_normed, w_up, preferred_element_type=jnp.float32)
    act = (jax.nn.silu(gate) * up).astype(jnp.bfloat16)
    hidden = (mid_f + jnp.dot(act, w_down, preferred_element_type=jnp.float32)).astype(jnp.bfloat16)
    return (hidden, key_matrix.reshape(PACKED_TOKENS, KEY_VALUE_HEADS * HEAD_DIM), value_matrix)
```

```python
import functools
import math

import jax
import jax.numpy as jnp
from jax import lax
from jax.experimental import pallas as pl
from jax.experimental.pallas import tpu as pltpu
from jax.sharding import PartitionSpec as P

F32 = jnp.float32
BF16 = jnp.bfloat16
EPS = 1e-06
VMEM_BYTES = 48 * 1024 * 1024


def rms(v, gain):
    return v * lax.rsqrt(jnp.mean(v * v, axis=-1, keepdims=True) + EPS) * gain


def rope_tables(positions, head):
    half = head // 2
    freqs = 1000000.0 ** (-2.0 * jnp.arange(half, dtype=F32) / head)
    angle = positions.astype(F32)[:, None] * freqs[None, :]
    c, s = jnp.cos(angle), jnp.sin(angle)
    return jnp.concatenate([c, c], axis=-1), jnp.concatenate([-s, s], axis=-1)


def call(kernel, out_shape, *args, scalars=(), any_args=0, scratch=(), flops=0, bytes_=0):
    n = len(args) - any_args
    in_specs = [pl.BlockSpec(memory_space=pltpu.SMEM)] * len(scalars)
    in_specs += [pl.BlockSpec(memory_space=pltpu.VMEM)] * n
    in_specs += [pl.BlockSpec(memory_space=pl.ANY)] * any_args
    many = isinstance(out_shape, (list, tuple))
    vm = pl.BlockSpec(memory_space=pltpu.VMEM)
    return pl.pallas_call(
        kernel,
        out_shape=out_shape,
        in_specs=in_specs,
        out_specs=[vm] * len(out_shape) if many else vm,
        scratch_shapes=list(scratch),
        compiler_params=pltpu.CompilerParams(vmem_limit_bytes=VMEM_BYTES),
        cost_estimate=pl.CostEstimate(flops=flops, bytes_accessed=bytes_, transcendentals=0),
    )(*scalars, *args)


def head_rope(v, gain, c, s):
    head = gain.shape[-1]
    out = []
    for h in range(v.shape[1] // head):
        n = rms(v[:, h * head : (h + 1) * head], gain)
        out.append((n * c + pltpu.roll(n, head // 2, 1) * s).astype(BF16))
    return jnp.concatenate(out, axis=1)


def kv_kernel(x_ref, gain_ref, kw_ref, vw_ref, kg_ref, c_ref, s_ref, n_ref, kv_ref, k_ref, v_ref):
    n = rms(x_ref[...].astype(F32), gain_ref[...]).astype(BF16)
    n_ref[...] = n
    width = kw_ref.shape[1]
    k = jnp.dot(n, kw_ref[...], preferred_element_type=F32)
    k = head_rope(k, kg_ref[...], c_ref[...], s_ref[...])
    v = jnp.dot(n, vw_ref[...], preferred_element_type=F32).astype(BF16)
    k_ref[...] = k
    v_ref[...] = v
    kv_ref[:, :width] = k
    kv_ref[:, width:] = v


def q_kernel(n_ref, w_ref, g_ref, c_ref, s_ref, q_ref):
    q = jnp.dot(n_ref[...], w_ref[...], preferred_element_type=F32)
    q_ref[...] = head_rope(q, g_ref[...], c_ref[...], s_ref[...])


def attention_kernel(head, kv_heads, sc_ref, pos_ref, q_ref, w_ref, *rest):
    blocks, (away_ref, own_ref, top, total, acc, att) = rest[:-6], rest[-6:]
    rows = q_ref.shape[0]
    group = q_ref.shape[1] // (head * kv_heads)
    me, first, core = sc_ref[0], sc_ref[1], sc_ref[2]
    scale = math.log2(math.e) / math.sqrt(head)
    query = me * rows + lax.broadcasted_iota(jnp.int32, (1, rows), 1)
    start = query - pos_ref[...]
    width = kv_heads * head

    def scores(g, ref, block):
        qs = [q_ref[:, (g * group + i) * head : (g * group + i + 1) * head] for i in range(group)]
        qg = jnp.concatenate(qs, axis=0)
        s = lax.dot_general(
            ref[:, g * head : (g + 1) * head], qg, (((1,), (1,)), ((), ())), preferred_element_type=F32
        )
        key = block * rows + lax.broadcasted_iota(jnp.int32, (rows, rows), 0)
        ok = (key >= start) & (key <= query)
        return jnp.where(jnp.concatenate([ok] * group, axis=1), s * scale, -1e30)

    def weigh(g, ref, p):
        return lax.dot_general(
            ref[:, width + g * head : width + (g + 1) * head],
            p.astype(BF16),
            (((0,), (0,)), ((), ())),
            preferred_element_type=F32,
        )

    for g in range(kv_heads):
        s = scores(g, blocks[0], me)
        m = jnp.max(s, axis=0, keepdims=True)
        p = jnp.exp2(s - m)
        top[g] = m
        total[g] = jnp.sum(p, axis=0, keepdims=True)
        acc[g] = weigh(g, blocks[0], p)

    for i, ref in enumerate(blocks[1:]):
        block = sc_ref[4 + i]

        @pl.when((block >= 0) & (block < me) & (block * rows + rows > first))
        def _():
            for g in range(kv_heads):
                s = scores(g, ref, block)
                old = top[g]
                m = jnp.maximum(old, jnp.max(s, axis=0, keepdims=True))
                p = jnp.exp2(s - m)
                decay = jnp.exp2(old - m)
                top[g] = m
                total[g] = total[g] * decay + jnp.sum(p, axis=0, keepdims=True)
                acc[g] = acc[g] * decay + weigh(g, ref, p)

    for g in range(kv_heads):
        a = (acc[g] / total[g]).T.astype(BF16)
        for i in range(group):
            h = g * group + i
            att[:, h * head : (h + 1) * head] = a[i * rows : (i + 1) * rows]
    half = rows // 2
    for ref, which in ((away_ref, 1 - core), (own_ref, core)):
        a = att[pl.ds(pl.multiple_of(which * half, half), half), :]
        ref[...] = jnp.dot(a, w_ref[...], preferred_element_type=F32).astype(ref.dtype)


def gate_kernel(sc_ref, own_ref, away_ref, gain_ref, *rest):
    pieces, (act_ref, wg, wu, sem) = rest[:-4], rest[-4:]
    rows = pieces[0].shape[0] // 2
    copies = []
    for i, piece in enumerate(pieces):
        at = pl.ds(pl.multiple_of(sc_ref[i] * rows, rows), rows)
        copies.append(pltpu.make_async_copy(piece.at[pl.ds(0, rows)], wg.at[at], sem.at[2 * i]))
        copies.append(pltpu.make_async_copy(piece.at[pl.ds(rows, rows)], wu.at[at], sem.at[2 * i + 1]))
    for copy in copies:
        copy.start()
    gain = gain_ref[...]
    n = jnp.concatenate(
        [rms(ref[...].astype(F32), gain).astype(BF16) for ref in (own_ref, away_ref)], axis=0
    )
    for copy in copies:
        copy.wait()
    gate = jnp.dot(n, wg[...], preferred_element_type=F32)
    up = jnp.dot(n, wu[...], preferred_element_type=F32)
    act_ref[...] = (gate / (1.0 + jnp.exp(-gate)) * up).astype(BF16)


def down_kernel(act_ref, *rest):
    pieces, (away_ref, own_ref) = rest[:-2], rest[-2:]
    half = act_ref.shape[0] // 2
    for i, piece in enumerate(pieces):
        wide = piece.shape[1]
        t = jnp.dot(act_ref[...], piece[...], preferred_element_type=F32)
        away_ref[:, i * wide : (i + 1) * wide] = t[half:].astype(BF16)
        own_ref[:, i * wide : (i + 1) * wide] = t[:half]


def last_sum_kernel(wide, sc_ref, mid_ref, a_ref, b_ref, out_ref):
    for i in range(a_ref.shape[1] // wide):
        here = slice(i * wide, (i + 1) * wide)
        mid = mid_ref[:, pl.ds(pl.multiple_of(sc_ref[i] * wide, wide), wide)].astype(F32)
        add = a_ref[:, here].astype(F32) + b_ref[:, here].astype(F32)
        out_ref[:, here] = (mid + add).astype(BF16)


def place_kernel(wide, sc_ref, *rest):
    pairs, out_ref = rest[:-1], rest[-1]
    core = sc_ref[0]
    at = 1
    for own_ref, away_ref in zip(pairs[0::2], pairs[1::2]):
        half = own_ref.shape[0]
        for i in range(own_ref.shape[1] // wide):
            cols = pl.ds(pl.multiple_of(sc_ref[at] * wide, wide), wide)
            here = slice(i * wide, (i + 1) * wide)
            out_ref[pl.ds(pl.multiple_of(core * half, half), half), cols] = own_ref[:, here]
            out_ref[pl.ds(pl.multiple_of((1 - core) * half, half), half), cols] = away_ref[:, here]
            at += 1


def grid_body(
    layer_input, norm_gain, w_query, key_weight, value_weight, w_out, query_gain, key_gain,
    seg_ids, positions, post_gain, w_gate, w_up, w_down,
):
    rows, model = layer_input.shape
    head = query_gain.shape[0]
    kv_heads = key_weight.shape[1] // head
    kv_width = key_weight.shape[1]
    me = lax.axis_index("seq")
    core = lax.axis_index("tp") % 2
    half = rows // 2
    sds = jax.ShapeDtypeStruct

    every = range(8)

    def swap_x(v, who=every):
        return lax.ppermute(v, "seq", [(s, s ^ 1) for s in who])

    def up(v, who=every):
        return lax.ppermute(v, "seq", [(s, (s + 2) % 8) for s in who])

    def down(v, who=every):
        return lax.ppermute(v, "seq", [(s, (s - 2) % 8) for s in who])

    def swap_core(v):
        return lax.ppermute(v, "tp", [(t, t ^ 1) for t in range(4)])

    def swap_y(v):
        return lax.ppermute(v, "tp", [(t, t ^ 2) for t in range(4)])

    def gather(v, far):
        x = swap_x(v)
        u, d = up(v), down(v)
        f = far(u, d)
        return [v, x, u, up(x), d, down(x), f, swap_x(f)]

    one = me ^ 1
    z_up, z_down, z_far = (me + 6) % 8, (me + 2) % 8, (me + 4) % 8
    order = [me, one, z_up, z_up ^ 1, z_down, z_down ^ 1, z_far, z_far ^ 1]

    gate_up = jnp.concatenate([w_gate, w_up], axis=0)
    gu = gather(gate_up, lambda u, d: up(u))

    c, s = rope_tables(positions, head)
    normed, kv, key_cache, value_cache = call(
        kv_kernel,
        [sds((rows, model), BF16), sds((rows, 2 * kv_width), BF16)] + [sds((rows, kv_width), BF16)] * 2,
        layer_input, norm_gain[None], key_weight, value_weight, key_gain[None], c, s,
        flops=4 * rows * model * kv_width, bytes_=8 * model * kv_width,
    )
    k_x = swap_x(kv, (0, 2, 4, 6))
    k_u = up(kv, range(6))
    k_w = down(kv, (0, 1))
    k_ux = swap_x(k_u, range(2, 8))
    k_2 = up(k_u, range(2, 6))
    k_wx = swap_x(k_w, (6, 7))
    k_2x = swap_x(k_2, range(4, 8))
    blocks = [kv, k_x, k_u, k_ux, k_2, k_2x, k_w, k_wx]
    ids = [me, jnp.where(me % 2 == 1, me - 1, -1), me - 2, (me - 2) ^ 1, me - 4, (me - 4) ^ 1]
    ids += [me - 6, (me - 6) ^ 1]
    q = call(
        q_kernel, sds((rows, w_query.shape[1]), BF16), normed, w_query, query_gain[None], c, s,
        flops=2 * rows * model * w_query.shape[1], bytes_=2 * model * w_query.shape[1],
    )
    wd = gather(w_down, lambda u, d: down(d))

    sc = jnp.stack([me, me * rows - positions[0], core] + ids).astype(jnp.int32)
    group_rows = rows * (w_query.shape[1] // kv_width)
    away, own = call(
        functools.partial(attention_kernel, head, kv_heads),
        [sds((half, model), BF16), sds((half, model), F32)],
        positions[None], q, w_out, *blocks,
        scalars=(sc,),
        scratch=[
            pltpu.VMEM((kv_heads, 1, group_rows), F32),
            pltpu.VMEM((kv_heads, 1, group_rows), F32),
            pltpu.VMEM((kv_heads, head, group_rows), F32),
            pltpu.VMEM((rows, w_query.shape[1]), BF16),
        ],
        flops=6 * 10**9, bytes_=8 * 10**6,
    )
    chip = (own + swap_core(away).astype(F32)).astype(BF16)
    other_chip = swap_y(chip)
    x_half = lax.dynamic_slice_in_dim(layer_input, core * half, half, 0)
    mid = (x_half.astype(F32) + (chip.astype(F32) + other_chip.astype(F32))).astype(BF16)
    mid_away = swap_core(mid)

    order_sc = jnp.stack(order).astype(jnp.int32)
    ff = w_gate.shape[1]
    act = call(
        gate_kernel, sds((rows, ff), BF16), mid, mid_away, post_gain[None], *gu,
        scalars=(order_sc,), any_args=8,
        scratch=[pltpu.VMEM((model, ff), BF16)] * 2 + [pltpu.SemaphoreType.DMA((16,))],
        flops=4 * rows * model * ff, bytes_=4 * model * ff,
    )
    wide = w_down.shape[1]
    pairs, placed = [], []
    for part in ([0, 1, 2, 3], [4, 5, 6, 7]):
        cols = len(part) * wide
        away, own = call(
            down_kernel, [sds((half, cols), BF16), sds((half, cols), F32)],
            act, *[wd[i] for i in part],
            flops=2 * rows * ff * cols, bytes_=2 * ff * cols,
        )
        chip = (own + swap_core(away).astype(F32)).astype(BF16)
        part_ids = [order[i] for i in part]
        done = call(
            functools.partial(last_sum_kernel, wide), sds((half, cols), BF16),
            mid, chip, swap_y(chip),
            scalars=(jnp.stack(part_ids).astype(jnp.int32),),
            flops=10 * half * cols, bytes_=8 * half * cols,
        )
        pairs += [done, swap_core(done)]
        placed += part_ids
    hidden = call(
        functools.partial(place_kernel, wide), sds((rows, model), BF16), *pairs,
        scalars=(jnp.stack([core] + placed).astype(jnp.int32),),
        flops=rows * model, bytes_=4 * rows * model,
    )
    return (hidden, key_cache, value_cache)


def rope(v, place):
    c, s = rope_tables(place, v.shape[-1])
    return v * c[:, None, :] + jnp.roll(v, v.shape[-1] // 2, axis=-1) * s[:, None, :]


def general_body(
    layer_input, norm_gain, w_query, key_weight, value_weight, w_out, query_gain, key_gain,
    seg_ids, positions, post_gain, w_gate, w_up, w_down,
):
    rows = layer_input.shape[0]
    head = query_gain.shape[0]
    kv_local = key_weight.shape[1] // head
    group = w_query.shape[1] // head // kv_local
    scale = 1.0 / math.sqrt(head)
    xf = layer_input.astype(F32)
    normed = rms(xf, norm_gain).astype(BF16)

    def heads(w, gain):
        v = jnp.dot(normed, w, preferred_element_type=F32).reshape(rows, -1, head)
        return rope(rms(v, gain), positions).astype(BF16)

    q = heads(w_query, query_gain).reshape(rows, kv_local, group, head).transpose(1, 2, 0, 3)
    key_cache = heads(key_weight, key_gain).reshape(rows, kv_local * head)
    value_cache = jnp.dot(normed, value_weight, preferred_element_type=F32).astype(BF16)
    me = lax.axis_index("seq")
    keys = lax.all_gather(key_cache, "seq", axis=0, tiled=True)
    values = lax.all_gather(value_cache, "seq", axis=0, tiled=True)
    query = me * rows + jnp.arange(rows, dtype=jnp.int32)
    start = query - positions
    width = rows * math.gcd(keys.shape[0] // rows, max(1, 1024 // rows))

    def update(state, kb, vb, offset):
        top, total, acc = state
        kb = kb.reshape(width, kv_local, head)
        s = jnp.einsum("hgqd,khd->hgqk", q, kb, preferred_element_type=F32) * scale
        key = offset + jnp.arange(width, dtype=jnp.int32)
        ok = (key[None, :] >= start[:, None]) & (key[None, :] <= query[:, None])
        s = jnp.where(ok, s, -1e30)
        new_top = jnp.maximum(top, jnp.max(s, axis=-1))
        p = jnp.where(ok, jnp.exp(s - new_top[..., None]), 0.0)
        decay = jnp.exp(top - new_top)
        vb = vb.reshape(width, kv_local, head)
        add = jnp.einsum("hgqk,khd->hgqd", p.astype(BF16), vb, preferred_element_type=F32)
        return (new_top, total * decay + jnp.sum(p, axis=-1), acc * decay[..., None] + add)

    def one_block(step, state):
        offset = step * width
        kb = lax.dynamic_slice_in_dim(keys, offset, width, 0)
        vb = lax.dynamic_slice_in_dim(values, offset, width, 0)
        skip = (offset > query[-1]) | (offset + width <= start[0])
        return lax.cond(skip, lambda c: c, lambda c: update(c, kb, vb, offset), state)

    state = (
        jnp.full((kv_local, group, rows), -1e30, F32),
        jnp.zeros((kv_local, group, rows), F32),
        jnp.zeros((kv_local, group, rows, head), F32),
    )
    top, total, acc = lax.fori_loop(0, keys.shape[0] // width, one_block, state)
    attended = (acc / total[..., None]).astype(BF16).transpose(2, 0, 1, 3).reshape(rows, -1)
    partial_out = jnp.dot(attended, w_out, preferred_element_type=F32)
    summed = lax.psum(partial_out.astype(BF16), "tp").astype(F32)
    mid = (xf + summed).astype(BF16)
    mid_f = mid.astype(F32)
    post_normed = rms(mid_f, post_gain).astype(BF16)
    gate_w = lax.all_gather(w_gate, "seq", axis=0, tiled=True)
    up_w = lax.all_gather(w_up, "seq", axis=0, tiled=True)
    down_w = lax.all_gather(w_down, "seq", axis=1, tiled=True)
    gate = jnp.dot(post_normed, gate_w, preferred_element_type=F32)
    up = jnp.dot(post_normed, up_w, preferred_element_type=F32)
    act = (jax.nn.silu(gate) * up).astype(BF16)
    terms = jnp.dot(act, down_w, preferred_element_type=F32)
    ffn_total = lax.psum(terms.astype(BF16), "tp").astype(F32)
    hidden = (mid_f + ffn_total).astype(BF16)
    return (hidden, key_cache, value_cache)


def solution(mesh):
    in_specs = (
        P("seq", None),
        P(),
        P(None, "tp"),
        P(None, "tp"),
        P(None, "tp"),
        P("tp", None),
        P(),
        P(),
        P("seq"),
        P("seq"),
        P(),
        P("seq", "tp"),
        P("seq", "tp"),
        P("tp", "seq"),
    )
    out_specs = (P("seq", None), P("seq", "tp"), P("seq", "tp"))
    body = grid_body if (mesh.shape["seq"], mesh.shape["tp"]) == (8, 4) else general_body
    return jax.shard_map(body, mesh=mesh, in_specs=in_specs, out_specs=out_specs, check_vma=False)
```

```python
import functools
import math

import jax
import jax.numpy as jnp
from jax import lax
from jax.experimental import pallas as pl
from jax.experimental.pallas import tpu as pltpu
from jax.sharding import PartitionSpec as P

F32 = jnp.float32
BF16 = jnp.bfloat16
EPS = 1e-06
VMEM_BYTES = 24 * 1024 * 1024


def rms(v, gain):
    return v * lax.rsqrt(jnp.mean(v * v, axis=-1, keepdims=True) + EPS) * gain


def rope_tables(positions, head):
    half = head // 2
    freqs = 1000000.0 ** (-2.0 * jnp.arange(half, dtype=F32) / head)
    angle = positions.astype(F32)[:, None] * freqs[None, :]
    c, s = jnp.cos(angle), jnp.sin(angle)
    return jnp.concatenate([c, c], axis=-1), jnp.concatenate([-s, s], axis=-1)


def call(kernel, out_shape, *args, scratch=()):
    vm = pl.BlockSpec(memory_space=pltpu.VMEM)
    many = isinstance(out_shape, (list, tuple))
    return pl.pallas_call(
        kernel,
        out_shape=out_shape,
        in_specs=[vm] * len(args),
        out_specs=[vm] * len(out_shape) if many else vm,
        scratch_shapes=list(scratch),
        compiler_params=pltpu.CompilerParams(vmem_limit_bytes=VMEM_BYTES),
        cost_estimate=pl.CostEstimate(flops=1, bytes_accessed=1, transcendentals=0),
    )(*args)


def head_rope(v, gain, c, s):
    head = gain.shape[-1]
    out = []
    for h in range(v.shape[1] // head):
        n = rms(v[:, h * head : (h + 1) * head], gain)
        out.append((n * c + pltpu.roll(n, head // 2, 1) * s).astype(BF16))
    return jnp.concatenate(out, axis=1)


def kv_kernel(x_ref, gain_ref, kw_ref, vw_ref, kg_ref, c_ref, s_ref, n_ref, kv_ref, k_ref, v_ref):
    n = rms(x_ref[...].astype(F32), gain_ref[...]).astype(BF16)
    n_ref[...] = n
    width = kw_ref.shape[1]
    k = jnp.dot(n, kw_ref[...], preferred_element_type=F32)
    k = head_rope(k, kg_ref[...], c_ref[...], s_ref[...])
    v = jnp.dot(n, vw_ref[...], preferred_element_type=F32).astype(BF16)
    k_ref[...] = k
    v_ref[...] = v
    kv_ref[:, :width] = k
    kv_ref[:, width:] = v


def q_kernel(n_ref, w_ref, g_ref, c_ref, s_ref, q_ref):
    q = jnp.dot(n_ref[...], w_ref[...], preferred_element_type=F32)
    q_ref[...] = head_rope(q, g_ref[...], c_ref[...], s_ref[...])


def attention_kernel(head, kv_heads, names, first, last, pos_ref, q_ref, *rest):
    rest = list(rest)
    carried = [] if first else [rest.pop(0) for _ in range(3)]
    blocks = [rest.pop(0) for _ in names]
    if last:
        out_ref = rest.pop(0)
    top, total, acc = rest
    rows = q_ref.shape[0]
    group = q_ref.shape[1] // (head * kv_heads)
    me = lax.axis_index("seq")
    scale = math.log2(math.e) / math.sqrt(head)
    query = me * rows + lax.broadcasted_iota(jnp.int32, (1, rows), 1)
    start = query - pos_ref[...]
    width = kv_heads * head

    def scores(g, ref, block):
        qs = [q_ref[:, (g * group + i) * head : (g * group + i + 1) * head] for i in range(group)]
        qg = jnp.concatenate(qs, axis=0)
        s = lax.dot_general(
            ref[:, g * head : (g + 1) * head], qg, (((1,), (1,)), ((), ())), preferred_element_type=F32
        )
        key = block * rows + lax.broadcasted_iota(jnp.int32, (rows, rows), 0)
        ok = (key >= start) & (key <= query)
        return jnp.where(jnp.concatenate([ok] * group, axis=1), s * scale, -1e30)

    def weigh(g, ref, p):
        return lax.dot_general(
            ref[:, width + g * head : width + (g + 1) * head],
            p.astype(BF16),
            (((0,), (0,)), ((), ())),
            preferred_element_type=F32,
        )

    for new, old in zip((top, total, acc), carried):
        new[...] = old[...]
    for i, ((name, swapped), ref) in enumerate(zip(names, blocks)):
        if first and i == 0:
            for g in range(kv_heads):
                s = scores(g, ref, me)
                m = jnp.max(s, axis=0, keepdims=True)
                p = jnp.exp2(s - m)
                top[g] = m
                total[g] = jnp.sum(p, axis=0, keepdims=True)
                acc[g] = weigh(g, ref, p)
            continue
        block = {"here": me, "pair": me - 2, "far": me - 4, "far pair": (me ^ 2) - 4}[name]
        there = (block >= 0) & ((me // 2) % 2 == 1 if name == "pair" else True)
        if swapped:
            block = block ^ 1

        @pl.when(there & (block < me))
        def _():
            for g in range(kv_heads):
                s = scores(g, ref, block)
                old = top[g]
                m = jnp.maximum(old, jnp.max(s, axis=0, keepdims=True))
                p = jnp.exp2(s - m)
                decay = jnp.exp2(old - m)
                top[g] = m
                total[g] = total[g] * decay + jnp.sum(p, axis=0, keepdims=True)
                acc[g] = acc[g] * decay + weigh(g, ref, p)

    if last:
        for g in range(kv_heads):
            a = (acc[g] / total[g]).T.astype(BF16)
            for i in range(group):
                h = g * group + i
                out_ref[:, h * head : (h + 1) * head] = a[i * rows : (i + 1) * rows]


def halves_kernel(gate_ref, up_ref, down_ref, *outs):
    rows, width = gate_ref.shape[0], outs[0].shape[1]
    keep = (lax.axis_index("seq") // 2) % 2
    for gu_ref, d_ref, which in (outs[:2] + (keep,), outs[2:] + (1 - keep,)):
        at = pl.ds(pl.multiple_of(which * width, 128), width)
        gu_ref[:rows, :] = gate_ref[:, at]
        gu_ref[rows:, :] = up_ref[:, at]
        d_ref[...] = down_ref[at, :]


def mid_kernel(x_ref, *rest):
    w, own, part, (mid_ref, sum_ref) = rest[:4], rest[4:8], rest[8:-2], rest[-2:]

    def product(blocks):
        total = None
        for w_ref, ref in zip(w, blocks):
            t = jnp.dot(ref[...], w_ref[...], preferred_element_type=F32)
            total = t if total is None else total + t
        return total

    mid_ref[...] = (x_ref[...].astype(F32) + product(own)).astype(BF16)
    sum_ref[...] = product(part)


def act_kernel(w2_ref, w3_ref, mid_ref, sum_ref, a2_ref, a3_ref, x_own_ref, x_away_ref, gain_ref, *rest):
    pieces, (act_ref, n_ref, v_ref) = rest[:8], rest[8:]
    rows = mid_ref.shape[0]
    half = rows // 2
    me = lax.axis_index("seq")
    core = lax.axis_index("tp") % 2
    keep = pl.ds(pl.multiple_of(core * half, half), half)
    away = pl.ds(pl.multiple_of((1 - core) * half, half), half)
    more = jnp.dot(a2_ref[...], w2_ref[...], preferred_element_type=F32)
    more += jnp.dot(a3_ref[...], w3_ref[...], preferred_element_type=F32)
    v_ref[...] = sum_ref[...] + more
    wide = pieces[0].shape[0] // 2
    blocks = [
        mid_ref[keep, :].astype(F32),
        (v_ref[keep, :] + x_own_ref[...].astype(F32)).astype(BF16).astype(F32),
        mid_ref[away, :].astype(F32),
        (v_ref[away, :] + x_away_ref[...].astype(F32)).astype(BF16).astype(F32),
    ]
    for i, v in enumerate(blocks):
        n = rms(v, gain_ref[...]).astype(BF16)
        n_ref[i * half : (i + 1) * half, :] = n
    n = jnp.concatenate(
        [n_ref[:, pl.ds(pl.multiple_of((me ^ k) * wide, wide), wide)] for k in range(8)], axis=1
    )
    wg = jnp.concatenate([ref[:wide, :] for ref in pieces], axis=0)
    wu = jnp.concatenate([ref[wide:, :] for ref in pieces], axis=0)
    gate = jnp.dot(n, wg, preferred_element_type=F32)
    up = jnp.dot(n, wu, preferred_element_type=F32)
    act_ref[...] = (gate / (1.0 + jnp.exp(-gate)) * up).astype(BF16)


def down_kernel(act_ref, *rest):
    pieces, (away_ref, keep_ref) = rest[:8], rest[8:]
    rows = act_ref.shape[0] // 2
    me = lax.axis_index("seq")
    for k, ref in enumerate(pieces):
        wide = ref.shape[1]
        cols = pl.ds(pl.multiple_of((me ^ k) * wide, wide), wide)
        t = jnp.dot(act_ref[...], ref[...], preferred_element_type=F32)
        keep_ref[:, cols] = t[:rows]
        away_ref[:, cols] = t[rows:].astype(BF16)


def split_sum_kernel(keep_ref, away_ref, own_ref, part_ref):
    half = own_ref.shape[0]
    own_ref[...] = (keep_ref[:half, :] + away_ref[:half, :].astype(F32)).astype(BF16)
    part_ref[...] = (keep_ref[half:, :] + away_ref[half:, :].astype(F32)).astype(BF16)


def pair_sum_kernel(a_ref, b_ref, out_ref):
    out_ref[...] = (a_ref[...].astype(F32) + b_ref[...].astype(F32)).astype(BF16)


def last_sum_kernel(mid_ref, a_ref, b_ref, out_ref):
    half = out_ref.shape[0]
    core = lax.axis_index("tp") % 2
    mid = mid_ref[pl.ds(pl.multiple_of(core * half, half), half), :]
    out_ref[...] = (mid.astype(F32) + (a_ref[...].astype(F32) + b_ref[...].astype(F32))).astype(BF16)


def place_kernel(keep_ref, away_ref, out_ref):
    half = keep_ref.shape[0]
    core = lax.axis_index("tp") % 2
    out_ref[pl.ds(pl.multiple_of(core * half, half), half), :] = keep_ref[...]
    out_ref[pl.ds(pl.multiple_of((1 - core) * half, half), half), :] = away_ref[...]


def grid_body(
    layer_input, norm_gain, w_query, key_weight, value_weight, w_out, query_gain, key_gain,
    seg_ids, positions, post_gain, w_gate, w_up, w_down,
):
    rows, model = layer_input.shape
    head = query_gain.shape[0]
    kv_heads = key_weight.shape[1] // head
    kv_width = key_weight.shape[1]
    me = lax.axis_index("seq")
    core = lax.axis_index("tp") % 2
    half = rows // 2
    ff = w_gate.shape[1] // 2
    sds = jax.ShapeDtypeStruct

    def swap(v, mask, who=range(8)):
        return lax.ppermute(v, "seq", [(a, a ^ mask) for a in who])

    def later(v, z, who=range(4)):
        return lax.ppermute(v, "seq", [(a, a + 2 * z) for a in who])

    def swap_tp(v, mask):
        return lax.ppermute(v, "tp", [(t, t ^ mask) for t in range(4)])

    def after(v, *results):
        return lax.optimization_barrier((v, results))[0]

    w_y, w_c = swap_tp(w_out, 2), swap_tp(w_out, 1)
    shape_g, shape_d = sds((2 * w_gate.shape[0], ff), BF16), sds((ff, w_down.shape[1]), BF16)
    g_mine, d_mine, g_theirs, d_theirs = call(
        halves_kernel, [shape_g, shape_d] * 2, w_gate, w_up, w_down
    )
    d4, d1 = swap(d_mine, 4), swap(d_mine, 1)
    x_half = lax.dynamic_slice_in_dim(layer_input, core * half, half, 0)

    c, s = rope_tables(positions, head)
    normed, kv, key_cache, value_cache = call(
        kv_kernel,
        [sds((rows, model), BF16), sds((rows, 2 * kv_width), BF16)] + [sds((rows, kv_width), BF16)] * 2,
        layer_input, norm_gain[None], key_weight, value_weight, key_gain[None], c, s,
    )
    k2, k1 = later(kv, 2), later(kv, 1, (0, 1, 4, 5))
    g_mine, g_theirs, kv_later = after((g_mine, g_theirs, kv), d4, d1)
    k0x = swap(kv_later, 1, (0, 2, 4, 6))
    g6 = swap(g_theirs, 6)
    k2, k1 = lax.optimization_barrier((k2, k1))
    k3 = swap(k2, 2, (4, 5, 6, 7))
    k2x = swap(k2, 1, (4, 5, 6, 7))
    k1x = swap(k1, 1, (2, 3, 6, 7))
    k3, k2x, k1x, k0x = lax.optimization_barrier((k3, k2x, k1x, k0x))
    k3x = swap(k3, 1, (4, 5, 6, 7))
    g2 = swap(after(g_theirs, k3), 2)
    g4 = swap(after(g_mine, k3), 4)
    q = call(
        q_kernel, sds((rows, w_query.shape[1]), BF16), normed, w_query, query_gain[None], c, s,
    )
    group_rows = rows * (w_query.shape[1] // kv_width)
    state = [sds((kv_heads, 1, group_rows), F32)] * 2 + [sds((kv_heads, head, group_rows), F32)]
    attend = functools.partial(attention_kernel, head, kv_heads)
    early = [("here", False), ("here", True), ("pair", False), ("pair", True)]
    early += [("far", False), ("far", True), ("far pair", False)]
    state = call(
        functools.partial(attend, early, True, False), state,
        positions[None], q, kv, k0x, k1, k1x, k2, k2x, k3,
    )
    k3x, g6, g2 = lax.optimization_barrier((k3x, g6, g2))
    a0 = call(
        functools.partial(attend, [("far pair", True)], False, True), sds((rows, w_query.shape[1]), BF16),
        positions[None], q, *state, k3x,
        scratch=[pltpu.VMEM(v.shape, F32) for v in state],
    )
    ay, az = swap_tp(a0, 2), swap(a0, 2)
    ac = swap_tp(a0, 1)
    xz = swap(x_half, 2)
    g6x = swap(g6, 1)
    g6x, g4, az, ay, xz = lax.optimization_barrier((g6x, g4, az, ay, xz))
    azy = swap(ay, 2)
    acy, acz = swap_tp(ay, 1), swap_tp(az, 1)
    g4x = swap(g4, 1)
    d6 = swap(after(d_theirs, az), 6)
    d2 = swap(after(d_theirs, az), 2)
    g2x = swap(g2, 1)
    acyz = swap_tp(azy, 1)
    xzc = swap_tp(xz, 1)
    g1 = swap(after(g_mine, azy), 1)
    d4x, d2x, d6x = swap(d4, 1), swap(d2, 1), swap(d6, 1)
    w_cy = swap_tp(w_y, 1)

    mid, part = call(
        mid_kernel, [sds((rows, model), BF16), sds((rows, model), F32)],
        layer_input, w_out, w_c, w_y, w_cy, a0, ac, ay, acy, az, acz,
    )
    act = call(
        act_kernel, sds((2 * rows, ff), BF16),
        w_y, w_cy, mid, part, azy, acyz, xz, xzc, post_gain[None], g_mine, g1, g2, g2x, g4, g4x, g6, g6x,
        scratch=[pltpu.VMEM((2 * rows, model), BF16), pltpu.VMEM((rows, model), F32)],
    )
    away, own = call(
        down_kernel, [sds((rows, model), BF16), sds((rows, model), F32)],
        act, d_mine, d1, d2, d2x, d4, d4x, d6, d6x,
    )
    mine, theirs = call(split_sum_kernel, [sds((half, model), BF16)] * 2, own, swap_tp(away, 1))
    chip = call(pair_sum_kernel, sds((half, model), BF16), mine, swap(theirs, 2))
    done = call(last_sum_kernel, sds((half, model), BF16), mid, chip, swap_tp(chip, 2))
    hidden = call(place_kernel, sds((rows, model), BF16), done, swap_tp(done, 1))
    return (hidden, key_cache, value_cache)


def rope(v, place):
    c, s = rope_tables(place, v.shape[-1])
    return v * c[:, None, :] + jnp.roll(v, v.shape[-1] // 2, axis=-1) * s[:, None, :]


def general_body(
    layer_input, norm_gain, w_query, key_weight, value_weight, w_out, query_gain, key_gain,
    seg_ids, positions, post_gain, w_gate, w_up, w_down,
):
    rows = layer_input.shape[0]
    head = query_gain.shape[0]
    kv_local = key_weight.shape[1] // head
    group = w_query.shape[1] // head // kv_local
    scale = 1.0 / math.sqrt(head)
    xf = layer_input.astype(F32)
    normed = rms(xf, norm_gain).astype(BF16)

    def heads(w, gain):
        v = jnp.dot(normed, w, preferred_element_type=F32).reshape(rows, -1, head)
        return rope(rms(v, gain), positions).astype(BF16)

    q = heads(w_query, query_gain).reshape(rows, kv_local, group, head).transpose(1, 2, 0, 3)
    key_cache = heads(key_weight, key_gain).reshape(rows, kv_local * head)
    value_cache = jnp.dot(normed, value_weight, preferred_element_type=F32).astype(BF16)
    me = lax.axis_index("seq")
    keys = lax.all_gather(key_cache, "seq", axis=0, tiled=True)
    values = lax.all_gather(value_cache, "seq", axis=0, tiled=True)
    query = me * rows + jnp.arange(rows, dtype=jnp.int32)
    start = query - positions
    width = rows * math.gcd(keys.shape[0] // rows, max(1, 1024 // rows))

    def update(state, kb, vb, offset):
        top, total, acc = state
        kb = kb.reshape(width, kv_local, head)
        s = jnp.einsum("hgqd,khd->hgqk", q, kb, preferred_element_type=F32) * scale
        key = offset + jnp.arange(width, dtype=jnp.int32)
        ok = (key[None, :] >= start[:, None]) & (key[None, :] <= query[:, None])
        s = jnp.where(ok, s, -1e30)
        new_top = jnp.maximum(top, jnp.max(s, axis=-1))
        p = jnp.where(ok, jnp.exp(s - new_top[..., None]), 0.0)
        decay = jnp.exp(top - new_top)
        vb = vb.reshape(width, kv_local, head)
        add = jnp.einsum("hgqk,khd->hgqd", p.astype(BF16), vb, preferred_element_type=F32)
        return (new_top, total * decay + jnp.sum(p, axis=-1), acc * decay[..., None] + add)

    def one_block(step, state):
        offset = step * width
        kb = lax.dynamic_slice_in_dim(keys, offset, width, 0)
        vb = lax.dynamic_slice_in_dim(values, offset, width, 0)
        skip = (offset > query[-1]) | (offset + width <= start[0])
        return lax.cond(skip, lambda c: c, lambda c: update(c, kb, vb, offset), state)

    state = (
        jnp.full((kv_local, group, rows), -1e30, F32),
        jnp.zeros((kv_local, group, rows), F32),
        jnp.zeros((kv_local, group, rows, head), F32),
    )
    top, total, acc = lax.fori_loop(0, keys.shape[0] // width, one_block, state)
    attended = (acc / total[..., None]).astype(BF16).transpose(2, 0, 1, 3).reshape(rows, -1)
    partial_out = jnp.dot(attended, w_out, preferred_element_type=F32)
    summed = lax.psum(partial_out.astype(BF16), "tp").astype(F32)
    mid = (xf + summed).astype(BF16)
    mid_f = mid.astype(F32)
    post_normed = rms(mid_f, post_gain).astype(BF16)
    gate_w = lax.all_gather(w_gate, "seq", axis=0, tiled=True)
    up_w = lax.all_gather(w_up, "seq", axis=0, tiled=True)
    down_w = lax.all_gather(w_down, "seq", axis=1, tiled=True)
    gate = jnp.dot(post_normed, gate_w, preferred_element_type=F32)
    up = jnp.dot(post_normed, up_w, preferred_element_type=F32)
    act = (jax.nn.silu(gate) * up).astype(BF16)
    terms = jnp.dot(act, down_w, preferred_element_type=F32)
    ffn_total = lax.psum(terms.astype(BF16), "tp").astype(F32)
    hidden = (mid_f + ffn_total).astype(BF16)
    return (hidden, key_cache, value_cache)


def solution(mesh):
    in_specs = (
        P("seq", None),
        P(),
        P(None, "tp"),
        P(None, "tp"),
        P(None, "tp"),
        P("tp", None),
        P(),
        P(),
        P("seq"),
        P("seq"),
        P(),
        P("seq", "tp"),
        P("seq", "tp"),
        P("tp", "seq"),
    )
    out_specs = (P("seq", None), P("seq", "tp"), P("seq", "tp"))
    body = grid_body if (mesh.shape["seq"], mesh.shape["tp"]) == (8, 4) else general_body
    return jax.shard_map(body, mesh=mesh, in_specs=in_specs, out_specs=out_specs, check_vma=False)
```

```python
import functools
import math

import jax
import jax.numpy as jnp
from jax import lax
from jax.experimental import pallas as pl
from jax.experimental.pallas import tpu as pltpu
from jax.sharding import PartitionSpec as P

F32 = jnp.float32
BF16 = jnp.bfloat16
EPS = 1e-06
VMEM_BYTES = 16 * 1024 * 1024
KV_VMEM_BYTES = 61 * 1024 * 1024
FIRST, OTHER = (0, 1, 2, 3), (4, 5, 6, 7)
PLAN = {'k1': (0, None),
 'k0x': (0, 2),
 'k1x': (None, None),
 'k2x': (None, None),
 'w1': (0, 4),
 'g6': (1, None),
 'g2': (2, 8),
 'g4': (2, None),
 'g6x': (7, None),
 'g2x': (None, 7),
 'g4x': (0, None),
 'd6': (7, 10),
 'd4': (6, 9),
 'd2': (7, None),
 'd6x': (None, None),
 'd4x': (8, None),
 'd2x': (None, None)}

def rms(v, gain):
    return v * lax.rsqrt(jnp.mean(v * v, axis=-1, keepdims=True) + EPS) * gain


def rope_table(positions, head):
    half = head // 2
    freqs = 1000000.0 ** (-2.0 * jnp.arange(half, dtype=F32) / head)
    angle = positions.astype(F32)[:, None] * freqs[None, :]
    return jnp.concatenate([jnp.cos(angle), jnp.sin(angle)], axis=-1)


def call(kernel, out_shape, *args, scratch=(), hbm=0, vmem=VMEM_BYTES):
    vm = pl.BlockSpec(memory_space=pltpu.VMEM)
    many = isinstance(out_shape, (list, tuple))
    return pl.pallas_call(
        kernel,
        out_shape=out_shape,
        in_specs=[pl.BlockSpec(memory_space=pltpu.HBM)] * hbm + [vm] * (len(args) - hbm),
        out_specs=[vm] * len(out_shape) if many else vm,
        scratch_shapes=list(scratch),
        compiler_params=pltpu.CompilerParams(vmem_limit_bytes=vmem),
        cost_estimate=pl.CostEstimate(flops=1, bytes_accessed=1, transcendentals=0),
    )(*args)


def head_rope(v, gain, table):
    head = gain.shape[-1]
    turned = pltpu.roll(table, head // 2, 1)
    first = lax.broadcasted_iota(jnp.int32, table.shape, 1) < head // 2
    c, s = jnp.where(first, table, turned), jnp.where(first, -turned, table)
    out = []
    for h in range(v.shape[1] // head):
        n = rms(v[:, h * head : (h + 1) * head], gain)
        out.append((n * c + pltpu.roll(n, head // 2, 1) * s).astype(BF16))
    return jnp.concatenate(out, axis=1)


def kv_kernel(*refs):
    srcs, (n_ref, kv_ref, k_ref, v_ref), bufs, sem = refs[:6], refs[6:10], refs[10:16], refs[16]
    copies = []
    for i, (src, buf) in enumerate(zip(srcs, bufs)):
        for j in range(2 if i < 4 else 1):
            part = src.shape[0] // 2 if i < 4 else 1
            at = pl.ds(j * part, part)
            copies.append(pltpu.make_async_copy(src.at[at], buf.at[at], sem.at[2 * i + j]))
    for copy in copies:
        copy.start()
    copies[8].wait()
    copies[9].wait()
    gain_ref, kg_ref = bufs[4:]
    x_ref, kw_ref, vw_ref, t_ref = bufs[:4]
    copies[0].wait()
    copies[1].wait()
    n = rms(x_ref[...].astype(F32), gain_ref[...]).astype(BF16)
    n_ref[...] = n
    width = kw_ref.shape[1]
    copies[2].wait()
    copies[3].wait()
    k = jnp.dot(n, kw_ref[...], preferred_element_type=F32)
    copies[6].wait()
    copies[7].wait()
    k = head_rope(k, kg_ref[...], t_ref[...])
    copies[4].wait()
    copies[5].wait()
    v = jnp.dot(n, vw_ref[...], preferred_element_type=F32).astype(BF16)
    k_ref[...] = k
    v_ref[...] = v
    kv_ref[:, :width] = k
    kv_ref[:, width:] = v


def q_kernel(n_ref, w_ref, g_ref, t_ref, q_ref):
    q = jnp.dot(n_ref[...], w_ref[...], preferred_element_type=F32)
    q_ref[...] = head_rope(q, g_ref[...], t_ref[...])


def attention_kernel(head, kv_heads, names, first, last, pos_ref, q_ref, *rest):
    rest = list(rest)
    carried = [] if first else [rest.pop(0) for _ in range(3)]
    blocks = [rest.pop(0) for _ in names]
    if last:
        out_ref = rest.pop(0)
    top, total, acc = rest
    rows = q_ref.shape[0]
    group = q_ref.shape[1] // (head * kv_heads)
    me = lax.axis_index("seq")
    scale = math.log2(math.e) / math.sqrt(head)
    query = me * rows + lax.broadcasted_iota(jnp.int32, (1, rows), 1)
    start = query - pos_ref[...]
    width = kv_heads * head

    def scores(g, ref, block):
        qs = [q_ref[:, (g * group + i) * head : (g * group + i + 1) * head] for i in range(group)]
        qg = jnp.concatenate(qs, axis=0)
        s = lax.dot_general(
            ref[:, g * head : (g + 1) * head], qg, (((1,), (1,)), ((), ())), preferred_element_type=F32
        )
        key = block * rows + lax.broadcasted_iota(jnp.int32, (rows, rows), 0)
        ok = (key >= start) & (key <= query)
        return jnp.where(jnp.concatenate([ok] * group, axis=1), s * scale, -1e30)

    def weigh(g, ref, p):
        return lax.dot_general(
            ref[:, width + g * head : width + (g + 1) * head],
            p.astype(BF16),
            (((0,), (0,)), ((), ())),
            preferred_element_type=F32,
        )

    for new, old in zip((top, total, acc), carried):
        new[...] = old[...]
    for i, ((name, swapped), ref) in enumerate(zip(names, blocks)):
        if first and i == 0:
            for g in range(kv_heads):
                s = scores(g, ref, me)
                m = jnp.max(s, axis=0, keepdims=True)
                p = jnp.exp2(s - m)
                top[g] = m
                total[g] = jnp.sum(p, axis=0, keepdims=True)
                acc[g] = weigh(g, ref, p)
            continue
        block = {"here": me, "pair": me - 2, "far": me - 4, "far pair": (me ^ 2) - 4}[name]
        there = (block >= 0) & ((me // 2) % 2 == 1 if name == "pair" else True)
        if swapped:
            block = block ^ 1

        @pl.when(there & (block < me))
        def _():
            for g in range(kv_heads):
                s = scores(g, ref, block)
                old = top[g]
                m = jnp.maximum(old, jnp.max(s, axis=0, keepdims=True))
                p = jnp.exp2(s - m)
                decay = jnp.exp2(old - m)
                top[g] = m
                total[g] = total[g] * decay + jnp.sum(p, axis=0, keepdims=True)
                acc[g] = acc[g] * decay + weigh(g, ref, p)

    if last:
        for g in range(kv_heads):
            a = (acc[g] / total[g]).T.astype(BF16)
            for i in range(group):
                h = g * group + i
                out_ref[:, h * head : (h + 1) * head] = a[i * rows : (i + 1) * rows]


def halves_kernel(gate_ref, up_ref, down_ref, *outs):
    rows, width = gate_ref.shape[0], outs[0].shape[1]
    keep = (lax.axis_index("seq") // 2) % 2
    for g_ref, d_ref, which in (outs[:2] + (keep,), outs[2:4] + (1 - keep,)):
        at = pl.ds(pl.multiple_of(which * width, 128), width)
        g_ref[:rows, :] = gate_ref[:, at]
        g_ref[rows:, :] = up_ref[:, at]
        d_ref[...] = down_ref[at, :].T
    outs[4][: 2 * rows, :] = outs[0][...]
    outs[4][2 * rows :, :] = outs[1][...]


def out_kernel(mine_ref, other_ref, w_mine_ref, w_other_ref, *outs):
    part = outs[0].shape[0]
    first = (lax.axis_index("tp") % 2) * 2 * part
    w = jnp.concatenate([w_mine_ref[...], w_other_ref[...]], axis=0)
    for i, out_ref in enumerate(outs):
        rows = pl.ds(pl.multiple_of(first + i * part, part), part)
        a = jnp.concatenate([mine_ref[rows, :], other_ref[rows, :]], axis=1)
        out_ref[...] = jnp.dot(a, w, preferred_element_type=F32).astype(BF16)


def mid_kernel(which, x_ref, a_ref, b_ref, mid_ref):
    part = mid_ref.shape[0]
    first = (lax.axis_index("tp") % 2) * 2 * part + which * part
    x = x_ref[pl.ds(pl.multiple_of(first, part), part), :]
    mid_ref[...] = (x.astype(F32) + (a_ref[...].astype(F32) + b_ref[...].astype(F32))).astype(BF16)


def act_kernel(*refs):
    blocks, gain_ref, pieces, (act_ref, n_ref) = refs[:8], refs[8], refs[9:17], refs[17:]
    part = blocks[0].shape[0]
    wide = pieces[2].shape[0] // 2
    me = lax.axis_index("seq")
    for i, ref in enumerate(blocks):
        n_ref[i * part : (i + 1) * part, :] = rms(ref[...].astype(F32), gain_ref[...]).astype(BF16)
    n = jnp.concatenate(
        [n_ref[:, pl.ds(pl.multiple_of((me ^ k) * wide, wide), wide)] for k in range(8)], axis=1
    )
    wg = jnp.concatenate([ref[:wide, :] for ref in pieces], axis=0)
    wu = jnp.concatenate([ref[wide : 2 * wide, :] for ref in pieces], axis=0)
    gate = jnp.dot(n, wg, preferred_element_type=F32)
    up = jnp.dot(n, wu, preferred_element_type=F32)
    act_ref[...] = (gate / (1.0 + jnp.exp(-gate)) * up).astype(BF16)


def down_kernel(act_ref, *rest):
    pieces, (away_ref, keep_ref) = rest[:-2], rest[-2:]
    rows = act_ref.shape[0] // 2
    wide = keep_ref.shape[1] // len(pieces)
    for i, ref in enumerate(pieces):
        cols = pl.ds(pl.multiple_of((i ^ (lax.axis_index("seq") & 2)) * wide, wide), wide)
        w = ref[ref.shape[0] - wide :, :]
        t = lax.dot_general(act_ref[...], w, (((1,), (1,)), ((), ())), preferred_element_type=F32)
        keep_ref[:, cols] = t[:rows]
        away_ref[:, cols] = t[rows:].astype(BF16)


def split_sum_kernel(keep_ref, away_ref, own_ref, part_ref):
    half = own_ref.shape[0]
    own_ref[...] = (keep_ref[:half, :].astype(F32) + away_ref[:half, :].astype(F32)).astype(BF16)
    part_ref[...] = (keep_ref[half:, :].astype(F32) + away_ref[half:, :].astype(F32)).astype(BF16)


def sum_kernel(a_ref, b_ref, out_ref):
    out_ref[...] = (a_ref[...].astype(F32) + b_ref[...].astype(F32)).astype(BF16)


def last_sum_kernel(shards, mid_a_ref, mid_b_ref, a_ref, b_ref, out_ref):
    wide = out_ref.shape[1] // len(shards)
    me = lax.axis_index("seq") & 5
    for i, k in enumerate(shards):
        here = slice(i * wide, (i + 1) * wide)
        cols = pl.ds(pl.multiple_of((me ^ k) * wide, wide), wide)
        mid = jnp.concatenate([mid_a_ref[:, cols], mid_b_ref[:, cols]], axis=0).astype(F32)
        add = a_ref[:, here].astype(F32) + b_ref[:, here].astype(F32)
        out_ref[:, here] = (mid + add).astype(BF16)


def place_kernel(parts, *rest):
    pairs, out_ref = rest[:-1], rest[-1]
    core = lax.axis_index("tp") % 2
    me = lax.axis_index("seq") & 5
    for shards, keep_ref, away_ref in zip(parts, pairs[0::2], pairs[1::2]):
        half = keep_ref.shape[0]
        wide = keep_ref.shape[1] // len(shards)
        for i, k in enumerate(shards):
            cols = pl.ds(pl.multiple_of((me ^ k) * wide, wide), wide)
            here = slice(i * wide, (i + 1) * wide)
            out_ref[pl.ds(pl.multiple_of(core * half, half), half), cols] = keep_ref[:, here]
            out_ref[pl.ds(pl.multiple_of((1 - core) * half, half), half), cols] = away_ref[:, here]


def grid_body(
    layer_input, norm_gain, w_query, key_weight, value_weight, w_out, query_gain, key_gain,
    seg_ids, positions, post_gain, w_gate, w_up, w_down,
):
    rows, model = layer_input.shape
    head = query_gain.shape[0]
    kv_heads = key_weight.shape[1] // head
    kv_width = key_weight.shape[1]
    me = lax.axis_index("seq")
    core = lax.axis_index("tp") % 2
    half = rows // 2
    ff = w_gate.shape[1] // 2
    sds = jax.ShapeDtypeStruct

    def send(name, v, axis, pairs):
        with jax.named_scope(name):
            return lax.ppermute(v, axis, pairs)

    def swap(name, v, mask, who=range(8)):
        return send(name, v, "seq", [(a, a ^ mask) for a in who])

    def later(name, v, z, who=range(4)):
        return send(name, v, "seq", [(a, a + 2 * z) for a in who])

    def swap_tp(name, v, mask):
        return send(name, v, "tp", [(t, t ^ mask) for t in range(4)])

    tie = lax.optimization_barrier
    reached = []

    def step(value):
        now = len(reached)
        here = [name for name in PLAN if PLAN[name][1] == now]
        value, there = tie((value, [get(name) for name in here]))
        sent.update(zip(here, there))
        reached.append(value)
        return value

    def get(name):
        if name not in sent:
            operand, send_one = transfers[name]
            operand = get(operand) if isinstance(operand, str) else operand
            after = PLAN[name][0]
            if after is not None:
                operand = tie((operand, reached[after]))[0]
            sent[name] = send_one(name, operand)
        return sent[name]

    sent = {}
    w_c = swap_tp("w_c", w_out, 1)
    table = rope_table(positions, head)
    normed, kv, key_cache, value_cache = call(
        kv_kernel,
        [sds((rows, model), BF16), sds((rows, 2 * kv_width), BF16)] + [sds((rows, kv_width), BF16)] * 2,
        layer_input, key_weight, value_weight, table, norm_gain[None], key_gain[None],
        scratch=[pltpu.VMEM(v.shape, v.dtype) for v in (layer_input, key_weight, value_weight, table)]
        + [pltpu.VMEM((1, v.shape[0]), F32) for v in (norm_gain, key_gain)]
        + [pltpu.SemaphoreType.DMA((12,))],
        hbm=6,
        vmem=KV_VMEM_BYTES,
    )
    w_late, w_c = tie((w_gate, kv, w_c))[::2]
    shapes = [sds((n * w_gate.shape[0], ff), BF16) for n in (2, 1, 3)]
    g_mine, d_mine, g_theirs, d_theirs, w_mine = call(
        halves_kernel, shapes[:2] * 2 + shapes[2:], w_late, w_up, w_down
    )
    q = call(
        q_kernel, sds((rows, w_query.shape[1]), BF16), normed, w_query, query_gain[None], table,
    )

    def along(mask, who=range(8)):
        return lambda name, v: swap(name, v, mask, who)

    transfers = {
        "k1": (kv, lambda name, v: later(name, v, 1, (0, 1, 4, 5))),
        "k0x": (kv, along(1, (0, 2, 4, 6))),
        "k1x": ("k1", along(1, (2, 3, 6, 7))),
        "k2x": ("k2", along(1, (4, 5, 6, 7))),
        "w1": (w_mine, along(1)),
        "g2": (g_theirs, along(2)),
        "g4": (g_mine, along(4)),
        "g6": (g_theirs, along(6)),
        "d2": (d_theirs, along(2)),
        "d4": (d_mine, along(4)),
        "d6": (d_theirs, along(6)),
        "g2x": ("g2", along(1)),
        "g4x": ("g4", along(1)),
        "g6x": ("g6", along(1)),
        "d2x": ("d2", along(1)),
        "d4x": ("d4", along(1)),
        "d6x": ("d6", along(1)),
    }
    kv_out = step(kv)
    k2 = later("k2", kv_out, 2)
    k2, q = tie((k2, q))
    k2 = sent["k2"] = step(k2)
    k3 = step(swap("k3", k2, 2, (4, 5, 6, 7)))
    group_rows = rows * (w_query.shape[1] // kv_width)
    state = [sds((kv_heads, 1, group_rows), F32)] * 2 + [sds((kv_heads, head, group_rows), F32)]
    attend = functools.partial(attention_kernel, head, kv_heads)
    early = [("here", False), ("pair", False), ("pair", True)]
    early += [("far", False), ("far", True), ("far pair", False)]
    k3x = swap("k3x", k3, 1, (4, 5, 6, 7))
    state = call(
        functools.partial(attend, early, True, False), state,
        positions[None], q, kv, get("k1"), get("k1x"), k2, get("k2x"), k3,
    )
    state = step(state)
    k3x = step(k3x)
    a0 = call(
        functools.partial(attend, [("here", True), ("far pair", True)], False, True),
        sds((rows, w_query.shape[1]), BF16),
        positions[None], q, *state, get("k0x"), k3x,
        scratch=[pltpu.VMEM(v.shape, F32) for v in state],
    )
    a0 = step(a0)
    quarter = sds((half // 2, model), BF16)
    outs = step(call(out_kernel, [quarter] * 2, a0, swap_tp("ac", a0, 1), w_out, w_c))
    out_ya, out_yb = swap_tp("out y a", outs[0], 2), swap_tp("out y b", outs[1], 2)
    out_ya = step(out_ya)
    mid_a = call(functools.partial(mid_kernel, 0), quarter, layer_input, outs[0], out_ya)
    part_a = swap("mid z a", mid_a, 2)
    mid_b = step(call(functools.partial(mid_kernel, 1), quarter, layer_input, outs[1], out_yb))
    part_b = step(swap("mid z b", mid_b, 2))
    rows_here = [mid_a, mid_b, part_a, part_b]
    rows_away = [swap_tp("rows core", v, 1) for v in rows_here]
    act = call(
        act_kernel, sds((2 * rows, ff), BF16),
        *rows_here, *rows_away, post_gain[None],
        g_mine, get("w1"), *[get(name) for name in ("g2", "g2x", "g4", "g4x", "g6", "g6x")],
        scratch=[pltpu.VMEM((2 * rows, model), BF16)],
    )
    act = step(act)
    wide = w_down.shape[1]
    downs = [d_mine, get("w1")] + [get(n) for n in ("d2", "d2x", "d4", "d4x", "d6", "d6x")]

    def down(shards, act):
        cols = len(shards) * wide
        away, own = call(
            down_kernel, [sds((rows, cols), BF16), sds((rows, cols), F32)],
            act, *[downs[k] for k in shards],
        )
        return own, swap_tp("sum core", away, 1)

    def last(shards, a, b):
        done = call(
            functools.partial(last_sum_kernel, shards), sds((half, len(shards) * wide), BF16), mid_a, mid_b, a, b
        )
        return [done, swap_tp("rows", done, 1)]

    own, away = down(FIRST, act)
    mine, theirs = call(split_sum_kernel, [sds((half, len(FIRST) * wide), BF16)] * 2, own, away)
    chip = call(sum_kernel, sds(mine.shape, BF16), mine, swap("sum z", theirs, 2))
    chip_y = swap_tp("sum y", chip, 2)
    own, away = down(OTHER, tie((act, mine))[0])
    both = call(sum_kernel, sds(own.shape, BF16), own, away)
    both_y = swap_tp("sum y", both, 2)
    mine, theirs = call(split_sum_kernel, [sds((half, len(OTHER) * wide), BF16)] * 2, both, both_y)
    pairs = last(FIRST, chip, chip_y) + last(OTHER, mine, swap("sum z", theirs, 2))
    hidden = call(functools.partial(place_kernel, (FIRST, OTHER)), sds((rows, model), BF16), *pairs)
    return (hidden, key_cache, value_cache)


def rope(v, place):
    half = v.shape[-1] // 2
    table = rope_table(place, v.shape[-1])[:, None, :]
    c, s = table[..., :half], table[..., half:]
    a, b = v[..., :half], v[..., half:]
    return jnp.concatenate([a * c - b * s, b * c + a * s], axis=-1)


def general_body(
    layer_input, norm_gain, w_query, key_weight, value_weight, w_out, query_gain, key_gain,
    seg_ids, positions, post_gain, w_gate, w_up, w_down,
):
    rows = layer_input.shape[0]
    head = query_gain.shape[0]
    kv_local = key_weight.shape[1] // head
    group = w_query.shape[1] // head // kv_local
    scale = 1.0 / math.sqrt(head)
    xf = layer_input.astype(F32)
    normed = rms(xf, norm_gain).astype(BF16)

    def heads(w, gain):
        v = jnp.dot(normed, w, preferred_element_type=F32).reshape(rows, -1, head)
        return rope(rms(v, gain), positions).astype(BF16)

    q = heads(w_query, query_gain).reshape(rows, kv_local, group, head).transpose(1, 2, 0, 3)
    key_cache = heads(key_weight, key_gain).reshape(rows, kv_local * head)
    value_cache = jnp.dot(normed, value_weight, preferred_element_type=F32).astype(BF16)
    me = lax.axis_index("seq")
    keys = lax.all_gather(key_cache, "seq", axis=0, tiled=True)
    values = lax.all_gather(value_cache, "seq", axis=0, tiled=True)
    query = me * rows + jnp.arange(rows, dtype=jnp.int32)
    start = query - positions
    width = rows * math.gcd(keys.shape[0] // rows, max(1, 1024 // rows))

    def update(state, kb, vb, offset):
        top, total, acc = state
        kb = kb.reshape(width, kv_local, head)
        s = jnp.einsum("hgqd,khd->hgqk", q, kb, preferred_element_type=F32) * scale
        key = offset + jnp.arange(width, dtype=jnp.int32)
        ok = (key[None, :] >= start[:, None]) & (key[None, :] <= query[:, None])
        s = jnp.where(ok, s, -1e30)
        new_top = jnp.maximum(top, jnp.max(s, axis=-1))
        p = jnp.where(ok, jnp.exp(s - new_top[..., None]), 0.0)
        decay = jnp.exp(top - new_top)
        vb = vb.reshape(width, kv_local, head)
        add = jnp.einsum("hgqk,khd->hgqd", p.astype(BF16), vb, preferred_element_type=F32)
        return (new_top, total * decay + jnp.sum(p, axis=-1), acc * decay[..., None] + add)

    def one_block(step, state):
        offset = step * width
        kb = lax.dynamic_slice_in_dim(keys, offset, width, 0)
        vb = lax.dynamic_slice_in_dim(values, offset, width, 0)
        skip = (offset > query[-1]) | (offset + width <= start[0])
        return lax.cond(skip, lambda c: c, lambda c: update(c, kb, vb, offset), state)

    state = (
        jnp.full((kv_local, group, rows), -1e30, F32),
        jnp.zeros((kv_local, group, rows), F32),
        jnp.zeros((kv_local, group, rows, head), F32),
    )
    top, total, acc = lax.fori_loop(0, keys.shape[0] // width, one_block, state)
    attended = (acc / total[..., None]).astype(BF16).transpose(2, 0, 1, 3).reshape(rows, -1)
    partial_out = jnp.dot(attended, w_out, preferred_element_type=F32)
    summed = lax.psum(partial_out.astype(BF16), "tp").astype(F32)
    mid = (xf + summed).astype(BF16)
    mid_f = mid.astype(F32)
    post_normed = rms(mid_f, post_gain).astype(BF16)
    gate_w = lax.all_gather(w_gate, "seq", axis=0, tiled=True)
    up_w = lax.all_gather(w_up, "seq", axis=0, tiled=True)
    down_w = lax.all_gather(w_down, "seq", axis=1, tiled=True)
    gate = jnp.dot(post_normed, gate_w, preferred_element_type=F32)
    up = jnp.dot(post_normed, up_w, preferred_element_type=F32)
    act = (jax.nn.silu(gate) * up).astype(BF16)
    terms = jnp.dot(act, down_w, preferred_element_type=F32)
    ffn_total = lax.psum(terms.astype(BF16), "tp").astype(F32)
    hidden = (mid_f + ffn_total).astype(BF16)
    return (hidden, key_cache, value_cache)


def solution(mesh):
    in_specs = (
        P("seq", None),
        P(),
        P(None, "tp"),
        P(None, "tp"),
        P(None, "tp"),
        P("tp", None),
        P(),
        P(),
        P("seq"),
        P("seq"),
        P(),
        P("seq", "tp"),
        P("seq", "tp"),
        P("tp", "seq"),
    )
    out_specs = (P("seq", None), P("seq", "tp"), P("seq", "tp"))
    body = grid_body if (mesh.shape["seq"], mesh.shape["tp"]) == (8, 4) else general_body
    return jax.shard_map(body, mesh=mesh, in_specs=in_specs, out_specs=out_specs, check_vma=False)
```

```python
import functools
import math

import jax
import jax.numpy as jnp
from jax import lax
from jax.experimental import pallas as pl
from jax.experimental.pallas import tpu as pltpu
from jax.sharding import PartitionSpec as P

F32 = jnp.float32
BF16 = jnp.bfloat16
EPS = 1e-06
VMEM_BYTES = 16 * 1024 * 1024
KV_VMEM_BYTES = 61 * 1024 * 1024
FIRST, OTHER = (0, 1, 2, 3, 4, 6), (5, 7)
PLAN = {'k1': (0, None),
 'k0x': (0, 2),
 'k1x': (None, None),
 'k2x': (None, None),
 'w1': (0, 4),
 'g6': (1, None),
 'g2': (2, 8),
 'g4': (2, None),
 'g6x': (7, None),
 'g2x': (None, 7),
 'g4x': (1, None),
 'd6': (7, 10),
 'd4': (6, 9),
 'd2': (7, None),
 'd6x': (None, None),
 'd4x': (8, None),
 'd2x': (None, None)}

def rms(v, gain):
    return v * lax.rsqrt(jnp.mean(v * v, axis=-1, keepdims=True) + EPS) * gain


def rope_table(positions, head):
    half = head // 2
    freqs = 1000000.0 ** (-2.0 * jnp.arange(half, dtype=F32) / head)
    angle = positions.astype(F32)[:, None] * freqs[None, :]
    return jnp.concatenate([jnp.cos(angle), jnp.sin(angle)], axis=-1)


def call(kernel, out_shape, *args, scratch=(), hbm=0, vmem=VMEM_BYTES):
    vm = pl.BlockSpec(memory_space=pltpu.VMEM)
    many = isinstance(out_shape, (list, tuple))
    return pl.pallas_call(
        kernel,
        out_shape=out_shape,
        in_specs=[pl.BlockSpec(memory_space=pltpu.HBM)] * hbm + [vm] * (len(args) - hbm),
        out_specs=[vm] * len(out_shape) if many else vm,
        scratch_shapes=list(scratch),
        compiler_params=pltpu.CompilerParams(vmem_limit_bytes=vmem),
        cost_estimate=pl.CostEstimate(flops=1, bytes_accessed=1, transcendentals=0),
    )(*args)


def head_rope(v, gain, table):
    head = gain.shape[-1]
    turned = pltpu.roll(table, head // 2, 1)
    first = lax.broadcasted_iota(jnp.int32, table.shape, 1) < head // 2
    c, s = jnp.where(first, table, turned), jnp.where(first, -turned, table)
    out = []
    for h in range(v.shape[1] // head):
        n = rms(v[:, h * head : (h + 1) * head], gain)
        out.append((n * c + pltpu.roll(n, head // 2, 1) * s).astype(BF16))
    return jnp.concatenate(out, axis=1)


def kv_kernel(*refs):
    srcs, (n_ref, kv_ref, k_ref, v_ref), bufs, sem = refs[:6], refs[6:10], refs[10:16], refs[16]
    copies = []
    for i, (src, buf) in enumerate(zip(srcs, bufs)):
        for j in range(2 if i < 4 else 1):
            part = src.shape[0] // 2 if i < 4 else 1
            at = pl.ds(j * part, part)
            copies.append(pltpu.make_async_copy(src.at[at], buf.at[at], sem.at[2 * i + j]))
    for copy in copies:
        copy.start()
    copies[8].wait()
    copies[9].wait()
    gain_ref, kg_ref = bufs[4:]
    x_ref, kw_ref, vw_ref, t_ref = bufs[:4]
    copies[0].wait()
    copies[1].wait()
    n = rms(x_ref[...].astype(F32), gain_ref[...]).astype(BF16)
    n_ref[...] = n
    width = kw_ref.shape[1]
    copies[2].wait()
    copies[3].wait()
    k = jnp.dot(n, kw_ref[...], preferred_element_type=F32)
    copies[6].wait()
    copies[7].wait()
    k = head_rope(k, kg_ref[...], t_ref[...])
    copies[4].wait()
    copies[5].wait()
    v = jnp.dot(n, vw_ref[...], preferred_element_type=F32).astype(BF16)
    k_ref[...] = k
    v_ref[...] = v
    kv_ref[:, :width] = k
    kv_ref[:, width:] = v


def q_kernel(n_ref, w_ref, g_ref, t_ref, q_ref):
    q = jnp.dot(n_ref[...], w_ref[...], preferred_element_type=F32)
    q_ref[...] = head_rope(q, g_ref[...], t_ref[...])


def attention_kernel(head, kv_heads, names, first, last, pos_ref, q_ref, *rest):
    rest = list(rest)
    carried = [] if first else [rest.pop(0) for _ in range(3)]
    blocks = [rest.pop(0) for _ in names]
    if last:
        out_ref = rest.pop(0)
    top, total, acc = rest
    rows = q_ref.shape[0]
    group = q_ref.shape[1] // (head * kv_heads)
    me = lax.axis_index("seq")
    scale = math.log2(math.e) / math.sqrt(head)
    query = me * rows + lax.broadcasted_iota(jnp.int32, (1, rows), 1)
    start = query - pos_ref[...]
    width = kv_heads * head

    def scores(g, ref, block):
        qs = [q_ref[:, (g * group + i) * head : (g * group + i + 1) * head] for i in range(group)]
        qg = jnp.concatenate(qs, axis=0)
        s = lax.dot_general(
            ref[:, g * head : (g + 1) * head], qg, (((1,), (1,)), ((), ())), preferred_element_type=F32
        )
        key = block * rows + lax.broadcasted_iota(jnp.int32, (rows, rows), 0)
        ok = (key >= start) & (key <= query)
        return jnp.where(jnp.concatenate([ok] * group, axis=1), s * scale, -1e30)

    def weigh(g, ref, p):
        return lax.dot_general(
            ref[:, width + g * head : width + (g + 1) * head],
            p.astype(BF16),
            (((0,), (0,)), ((), ())),
            preferred_element_type=F32,
        )

    for new, old in zip((top, total, acc), carried):
        new[...] = old[...]
    for i, ((name, swapped), ref) in enumerate(zip(names, blocks)):
        if first and i == 0:
            for g in range(kv_heads):
                s = scores(g, ref, me)
                m = jnp.max(s, axis=0, keepdims=True)
                p = jnp.exp2(s - m)
                top[g] = m
                total[g] = jnp.sum(p, axis=0, keepdims=True)
                acc[g] = weigh(g, ref, p)
            continue
        block = {"here": me, "pair": me - 2, "far": me - 4, "far pair": (me ^ 2) - 4}[name]
        there = (block >= 0) & ((me // 2) % 2 == 1 if name == "pair" else True)
        if swapped:
            block = block ^ 1

        @pl.when(there & (block < me))
        def _():
            for g in range(kv_heads):
                s = scores(g, ref, block)
                old = top[g]
                m = jnp.maximum(old, jnp.max(s, axis=0, keepdims=True))
                p = jnp.exp2(s - m)
                decay = jnp.exp2(old - m)
                top[g] = m
                total[g] = total[g] * decay + jnp.sum(p, axis=0, keepdims=True)
                acc[g] = acc[g] * decay + weigh(g, ref, p)

    if last:
        for g in range(kv_heads):
            a = (acc[g] / total[g]).T.astype(BF16)
            for i in range(group):
                h = g * group + i
                out_ref[:, h * head : (h + 1) * head] = a[i * rows : (i + 1) * rows]


def halves_kernel(gate_ref, up_ref, down_ref, *outs):
    rows, width = gate_ref.shape[0], outs[0].shape[1]
    keep = (lax.axis_index("seq") // 2) % 2
    for g_ref, d_ref, which in (outs[:2] + (keep,), outs[2:4] + (1 - keep,)):
        at = pl.ds(pl.multiple_of(which * width, 128), width)
        g_ref[:rows, :] = gate_ref[:, at]
        g_ref[rows:, :] = up_ref[:, at]
        d_ref[...] = down_ref[at, :].T
    outs[4][: 2 * rows, :] = outs[0][...]
    outs[4][2 * rows :, :] = outs[1][...]


def out_kernel(mine_ref, other_ref, w_mine_ref, w_other_ref, *outs):
    part = outs[0].shape[0]
    first = (lax.axis_index("tp") % 2) * 2 * part
    w = jnp.concatenate([w_mine_ref[...], w_other_ref[...]], axis=0)
    for i, out_ref in enumerate(outs):
        rows = pl.ds(pl.multiple_of(first + i * part, part), part)
        a = jnp.concatenate([mine_ref[rows, :], other_ref[rows, :]], axis=1)
        out_ref[...] = jnp.dot(a, w, preferred_element_type=F32).astype(BF16)


def mid_kernel(which, x_ref, a_ref, b_ref, mid_ref):
    part = mid_ref.shape[0]
    first = (lax.axis_index("tp") % 2) * 2 * part + which * part
    x = x_ref[pl.ds(pl.multiple_of(first, part), part), :]
    mid_ref[...] = (x.astype(F32) + (a_ref[...].astype(F32) + b_ref[...].astype(F32))).astype(BF16)


def act_kernel(*refs):
    blocks, gain_ref, pieces, (act_ref, n_ref) = refs[:8], refs[8], refs[9:17], refs[17:]
    part = blocks[0].shape[0]
    wide = pieces[2].shape[0] // 2
    me = lax.axis_index("seq")
    for i, ref in enumerate(blocks):
        n_ref[i * part : (i + 1) * part, :] = rms(ref[...].astype(F32), gain_ref[...]).astype(BF16)
    n = jnp.concatenate(
        [n_ref[:, pl.ds(pl.multiple_of((me ^ k) * wide, wide), wide)] for k in range(8)], axis=1
    )
    wg = jnp.concatenate([ref[:wide, :] for ref in pieces], axis=0)
    wu = jnp.concatenate([ref[wide : 2 * wide, :] for ref in pieces], axis=0)
    gate = jnp.dot(n, wg, preferred_element_type=F32)
    up = jnp.dot(n, wu, preferred_element_type=F32)
    act_ref[...] = (gate / (1.0 + jnp.exp(-gate)) * up).astype(BF16)


def down_kernel(shards, act_ref, *rest):
    pieces, (away_ref, keep_ref) = rest[:-2], rest[-2:]
    rows = act_ref.shape[0] // 2
    wide = keep_ref.shape[1] // len(pieces)
    for i, ref in enumerate(pieces):
        other = shards.index(shards[i] ^ 2)
        at = i + (lax.axis_index("seq") // 2) % 2 * (other - i)
        cols = pl.ds(pl.multiple_of(at * wide, wide), wide)
        w = ref[ref.shape[0] - wide :, :]
        t = lax.dot_general(act_ref[...], w, (((1,), (1,)), ((), ())), preferred_element_type=F32)
        keep_ref[:, cols] = t[:rows]
        away_ref[:, cols] = t[rows:].astype(BF16)


def split_sum_kernel(keep_ref, away_ref, own_ref, part_ref):
    half = own_ref.shape[0]
    own_ref[...] = (keep_ref[:half, :].astype(F32) + away_ref[:half, :].astype(F32)).astype(BF16)
    part_ref[...] = (keep_ref[half:, :].astype(F32) + away_ref[half:, :].astype(F32)).astype(BF16)


def sum_kernel(a_ref, b_ref, out_ref):
    out_ref[...] = (a_ref[...].astype(F32) + b_ref[...].astype(F32)).astype(BF16)


def last_sum_kernel(shards, mid_a_ref, mid_b_ref, a_ref, b_ref, out_ref):
    wide = out_ref.shape[1] // len(shards)
    me = lax.axis_index("seq") & 5
    for i, k in enumerate(shards):
        here = slice(i * wide, (i + 1) * wide)
        cols = pl.ds(pl.multiple_of((me ^ k) * wide, wide), wide)
        mid = jnp.concatenate([mid_a_ref[:, cols], mid_b_ref[:, cols]], axis=0).astype(F32)
        add = a_ref[:, here].astype(F32) + b_ref[:, here].astype(F32)
        out_ref[:, here] = (mid + add).astype(BF16)


def place_kernel(parts, *rest):
    pairs, out_ref = rest[:-1], rest[-1]
    core = lax.axis_index("tp") % 2
    me = lax.axis_index("seq") & 5
    for shards, keep_ref, away_ref in zip(parts, pairs[0::2], pairs[1::2]):
        half = keep_ref.shape[0]
        wide = keep_ref.shape[1] // len(shards)
        for i, k in enumerate(shards):
            cols = pl.ds(pl.multiple_of((me ^ k) * wide, wide), wide)
            here = slice(i * wide, (i + 1) * wide)
            out_ref[pl.ds(pl.multiple_of(core * half, half), half), cols] = keep_ref[:, here]
            out_ref[pl.ds(pl.multiple_of((1 - core) * half, half), half), cols] = away_ref[:, here]


def grid_body(
    layer_input, norm_gain, w_query, key_weight, value_weight, w_out, query_gain, key_gain,
    seg_ids, positions, post_gain, w_gate, w_up, w_down,
):
    rows, model = layer_input.shape
    head = query_gain.shape[0]
    kv_heads = key_weight.shape[1] // head
    kv_width = key_weight.shape[1]
    me = lax.axis_index("seq")
    core = lax.axis_index("tp") % 2
    half = rows // 2
    ff = w_gate.shape[1] // 2
    sds = jax.ShapeDtypeStruct

    def send(name, v, axis, pairs):
        with jax.named_scope(name):
            return lax.ppermute(v, axis, pairs)

    def swap(name, v, mask, who=range(8)):
        return send(name, v, "seq", [(a, a ^ mask) for a in who])

    def later(name, v, z, who=range(4)):
        return send(name, v, "seq", [(a, a + 2 * z) for a in who])

    def swap_tp(name, v, mask):
        return send(name, v, "tp", [(t, t ^ mask) for t in range(4)])

    tie = lax.optimization_barrier
    reached = []

    def step(value):
        now = len(reached)
        here = [name for name in PLAN if PLAN[name][1] == now]
        value, there = tie((value, [get(name) for name in here]))
        sent.update(zip(here, there))
        reached.append(value)
        return value

    def get(name):
        if name not in sent:
            operand, send_one = transfers[name]
            operand = get(operand) if isinstance(operand, str) else operand
            after = PLAN[name][0]
            if after is not None:
                operand = tie((operand, reached[after]))[0]
            sent[name] = send_one(name, operand)
        return sent[name]

    sent = {}
    w_c = swap_tp("w_c", w_out, 1)
    table = rope_table(positions, head)
    normed, kv, key_cache, value_cache = call(
        kv_kernel,
        [sds((rows, model), BF16), sds((rows, 2 * kv_width), BF16)] + [sds((rows, kv_width), BF16)] * 2,
        layer_input, key_weight, value_weight, table, norm_gain[None], key_gain[None],
        scratch=[pltpu.VMEM(v.shape, v.dtype) for v in (layer_input, key_weight, value_weight, table)]
        + [pltpu.VMEM((1, v.shape[0]), F32) for v in (norm_gain, key_gain)]
        + [pltpu.SemaphoreType.DMA((12,))],
        hbm=6,
        vmem=KV_VMEM_BYTES,
    )
    w_late, w_c = tie((w_gate, kv, w_c))[::2]
    shapes = [sds((n * w_gate.shape[0], ff), BF16) for n in (2, 1, 3)]
    g_mine, d_mine, g_theirs, d_theirs, w_mine = call(
        halves_kernel, shapes[:2] * 2 + shapes[2:], w_late, w_up, w_down
    )
    q = call(
        q_kernel, sds((rows, w_query.shape[1]), BF16), normed, w_query, query_gain[None], table,
    )

    def along(mask, who=range(8)):
        return lambda name, v: swap(name, v, mask, who)

    transfers = {
        "k1": (kv, lambda name, v: later(name, v, 1, (0, 1, 4, 5))),
        "k0x": (kv, along(1, (0, 2, 4, 6))),
        "k1x": ("k1", along(1, (2, 3, 6, 7))),
        "k2x": ("k2", along(1, (4, 5, 6, 7))),
        "w1": (w_mine, along(1)),
        "g2": (g_theirs, along(2)),
        "g4": (g_mine, along(4)),
        "g6": (g_theirs, along(6)),
        "d2": (d_theirs, along(2)),
        "d4": (d_mine, along(4)),
        "d6": (d_theirs, along(6)),
        "g2x": ("g2", along(1)),
        "g4x": ("g4", along(1)),
        "g6x": ("g6", along(1)),
        "d2x": ("d2", along(1)),
        "d4x": ("d4", along(1)),
        "d6x": ("d6", along(1)),
    }
    kv_out = step(kv)
    k2 = later("k2", kv_out, 2)
    k2, q = tie((k2, q))
    k2 = sent["k2"] = step(k2)
    k3 = step(swap("k3", k2, 2, (4, 5, 6, 7)))
    group_rows = rows * (w_query.shape[1] // kv_width)
    state = [sds((kv_heads, 1, group_rows), F32)] * 2 + [sds((kv_heads, head, group_rows), F32)]
    attend = functools.partial(attention_kernel, head, kv_heads)
    early = [("here", False), ("pair", False), ("pair", True)]
    early += [("far", False), ("far", True), ("far pair", False)]
    k3x = swap("k3x", k3, 1, (4, 5, 6, 7))
    state = call(
        functools.partial(attend, early, True, False), state,
        positions[None], q, kv, get("k1"), get("k1x"), k2, get("k2x"), k3,
    )
    state = step(state)
    k3x = step(k3x)
    a0 = call(
        functools.partial(attend, [("here", True), ("far pair", True)], False, True),
        sds((rows, w_query.shape[1]), BF16),
        positions[None], q, *state, get("k0x"), k3x,
        scratch=[pltpu.VMEM(v.shape, F32) for v in state],
    )
    a0 = step(a0)
    quarter = sds((half // 2, model), BF16)
    outs = step(call(out_kernel, [quarter] * 2, a0, swap_tp("ac", a0, 1), w_out, w_c))
    out_ya, out_yb = swap_tp("out y a", outs[0], 2), swap_tp("out y b", outs[1], 2)
    out_ya = step(out_ya)
    mid_a = call(functools.partial(mid_kernel, 0), quarter, layer_input, outs[0], out_ya)
    part_a = swap("mid z a", mid_a, 2)
    mid_b = step(call(functools.partial(mid_kernel, 1), quarter, layer_input, outs[1], out_yb))
    part_b = step(swap("mid z b", mid_b, 2))
    rows_here = [mid_a, mid_b, part_a, part_b]
    rows_away = [swap_tp("rows core", v, 1) for v in rows_here]
    act = call(
        act_kernel, sds((2 * rows, ff), BF16),
        *rows_here, *rows_away, post_gain[None],
        g_mine, get("w1"), *[get(name) for name in ("g2", "g2x", "g4", "g4x", "g6", "g6x")],
        scratch=[pltpu.VMEM((2 * rows, model), BF16)],
    )
    act = step(act)
    wide = w_down.shape[1]
    downs = [d_mine, get("w1")] + [get(n) for n in ("d2", "d2x", "d4", "d4x", "d6", "d6x")]

    def down(shards, act):
        cols = len(shards) * wide
        away, own = call(
            functools.partial(down_kernel, shards), [sds((rows, cols), BF16), sds((rows, cols), F32)],
            act, *[downs[k] for k in shards],
        )
        return own, swap_tp("sum core", away, 1)

    def last(shards, a, b):
        done = call(
            functools.partial(last_sum_kernel, shards), sds((half, len(shards) * wide), BF16), mid_a, mid_b, a, b
        )
        return [done, swap_tp("rows", done, 1)]

    def over_z(shards, act):
        own, away = down(shards, act)
        mine, theirs = call(split_sum_kernel, [sds((half, len(shards) * wide), BF16)] * 2, own, away)
        return call(sum_kernel, sds(mine.shape, BF16), mine, swap("sum z", theirs, 2))

    chip = over_z(FIRST, act)
    act, chip = tie((act, chip))
    pairs = last(FIRST, chip, swap_tp("sum y", chip, 2))
    chip = over_z(OTHER, act)
    pairs += last(OTHER, chip, swap_tp("sum y", chip, 2))
    hidden = call(functools.partial(place_kernel, (FIRST, OTHER)), sds((rows, model), BF16), *pairs)
    return (hidden, key_cache, value_cache)


def rope(v, place):
    half = v.shape[-1] // 2
    table = rope_table(place, v.shape[-1])[:, None, :]
    c, s = table[..., :half], table[..., half:]
    a, b = v[..., :half], v[..., half:]
    return jnp.concatenate([a * c - b * s, b * c + a * s], axis=-1)


def general_body(
    layer_input, norm_gain, w_query, key_weight, value_weight, w_out, query_gain, key_gain,
    seg_ids, positions, post_gain, w_gate, w_up, w_down,
):
    rows = layer_input.shape[0]
    head = query_gain.shape[0]
    kv_local = key_weight.shape[1] // head
    group = w_query.shape[1] // head // kv_local
    scale = 1.0 / math.sqrt(head)
    xf = layer_input.astype(F32)
    normed = rms(xf, norm_gain).astype(BF16)

    def heads(w, gain):
        v = jnp.dot(normed, w, preferred_element_type=F32).reshape(rows, -1, head)
        return rope(rms(v, gain), positions).astype(BF16)

    q = heads(w_query, query_gain).reshape(rows, kv_local, group, head).transpose(1, 2, 0, 3)
    key_cache = heads(key_weight, key_gain).reshape(rows, kv_local * head)
    value_cache = jnp.dot(normed, value_weight, preferred_element_type=F32).astype(BF16)
    me = lax.axis_index("seq")
    keys = lax.all_gather(key_cache, "seq", axis=0, tiled=True)
    values = lax.all_gather(value_cache, "seq", axis=0, tiled=True)
    query = me * rows + jnp.arange(rows, dtype=jnp.int32)
    start = query - positions
    width = rows * math.gcd(keys.shape[0] // rows, max(1, 1024 // rows))

    def update(state, kb, vb, offset):
        top, total, acc = state
        kb = kb.reshape(width, kv_local, head)
        s = jnp.einsum("hgqd,khd->hgqk", q, kb, preferred_element_type=F32) * scale
        key = offset + jnp.arange(width, dtype=jnp.int32)
        ok = (key[None, :] >= start[:, None]) & (key[None, :] <= query[:, None])
        s = jnp.where(ok, s, -1e30)
        new_top = jnp.maximum(top, jnp.max(s, axis=-1))
        p = jnp.where(ok, jnp.exp(s - new_top[..., None]), 0.0)
        decay = jnp.exp(top - new_top)
        vb = vb.reshape(width, kv_local, head)
        add = jnp.einsum("hgqk,khd->hgqd", p.astype(BF16), vb, preferred_element_type=F32)
        return (new_top, total * decay + jnp.sum(p, axis=-1), acc * decay[..., None] + add)

    def one_block(step, state):
        offset = step * width
        kb = lax.dynamic_slice_in_dim(keys, offset, width, 0)
        vb = lax.dynamic_slice_in_dim(values, offset, width, 0)
        skip = (offset > query[-1]) | (offset + width <= start[0])
        return lax.cond(skip, lambda c: c, lambda c: update(c, kb, vb, offset), state)

    state = (
        jnp.full((kv_local, group, rows), -1e30, F32),
        jnp.zeros((kv_local, group, rows), F32),
        jnp.zeros((kv_local, group, rows, head), F32),
    )
    top, total, acc = lax.fori_loop(0, keys.shape[0] // width, one_block, state)
    attended = (acc / total[..., None]).astype(BF16).transpose(2, 0, 1, 3).reshape(rows, -1)
    partial_out = jnp.dot(attended, w_out, preferred_element_type=F32)
    summed = lax.psum(partial_out.astype(BF16), "tp").astype(F32)
    mid = (xf + summed).astype(BF16)
    mid_f = mid.astype(F32)
    post_normed = rms(mid_f, post_gain).astype(BF16)
    gate_w = lax.all_gather(w_gate, "seq", axis=0, tiled=True)
    up_w = lax.all_gather(w_up, "seq", axis=0, tiled=True)
    down_w = lax.all_gather(w_down, "seq", axis=1, tiled=True)
    gate = jnp.dot(post_normed, gate_w, preferred_element_type=F32)
    up = jnp.dot(post_normed, up_w, preferred_element_type=F32)
    act = (jax.nn.silu(gate) * up).astype(BF16)
    terms = jnp.dot(act, down_w, preferred_element_type=F32)
    ffn_total = lax.psum(terms.astype(BF16), "tp").astype(F32)
    hidden = (mid_f + ffn_total).astype(BF16)
    return (hidden, key_cache, value_cache)


def solution(mesh):
    in_specs = (
        P("seq", None),
        P(),
        P(None, "tp"),
        P(None, "tp"),
        P(None, "tp"),
        P("tp", None),
        P(),
        P(),
        P("seq"),
        P("seq"),
        P(),
        P("seq", "tp"),
        P("seq", "tp"),
        P("tp", "seq"),
    )
    out_specs = (P("seq", None), P("seq", "tp"), P("seq", "tp"))
    body = grid_body if (mesh.shape["seq"], mesh.shape["tp"]) == (8, 4) else general_body
    return jax.shard_map(body, mesh=mesh, in_specs=in_specs, out_specs=out_specs, check_vma=False)
```

```python
import functools
import math

import jax
import jax.numpy as jnp
from jax import lax
from jax.experimental import pallas as pl
from jax.experimental.pallas import tpu as pltpu
from jax.sharding import PartitionSpec as P

F32 = jnp.float32
BF16 = jnp.bfloat16
EPS = 1e-06
VMEM_BYTES = 16 * 1024 * 1024
KV_VMEM_BYTES = 57 * 1024 * 1024
FIRST, OTHER = (0, 1, 2, 3, 4, 6), (5, 7)
PLAN = {'k1': (0, None),
 'k0x': (0, 2),
 'k1x': (None, None),
 'k2x': (None, None),
 'w1': (0, 4),
 'g6': (None, None),
 'g2': (2, 8),
 'g4': (2, None),
 'g6x': (7, None),
 'g2x': (None, 7),
 'g4x': (1, None),
 'd6': (5, 10),
 'd4': (6, 9),
 'd2': (7, None),
 'd6x': (None, None),
 'd4x': (1, None),
 'd2x': (None, None)}

def rms(v, gain):
    return v * lax.rsqrt(jnp.mean(v * v, axis=-1, keepdims=True) + EPS) * gain


def rope_table(positions, head):
    half = head // 2
    freqs = 1000000.0 ** (-2.0 * jnp.arange(half, dtype=F32) / head)
    angle = positions.astype(F32)[:, None] * freqs[None, :]
    return jnp.concatenate([jnp.cos(angle), jnp.sin(angle)], axis=-1)


def call(kernel, out_shape, *args, scratch=(), hbm=0, vmem=VMEM_BYTES):
    vm = pl.BlockSpec(memory_space=pltpu.VMEM)
    many = isinstance(out_shape, (list, tuple))
    return pl.pallas_call(
        kernel,
        out_shape=out_shape,
        in_specs=[pl.BlockSpec(memory_space=pltpu.HBM)] * hbm + [vm] * (len(args) - hbm),
        out_specs=[vm] * len(out_shape) if many else vm,
        scratch_shapes=list(scratch),
        compiler_params=pltpu.CompilerParams(vmem_limit_bytes=vmem),
        cost_estimate=pl.CostEstimate(flops=1, bytes_accessed=1, transcendentals=0),
    )(*args)


def head_rope(v, gain, table):
    head = gain.shape[-1]
    turned = pltpu.roll(table, head // 2, 1)
    first = lax.broadcasted_iota(jnp.int32, table.shape, 1) < head // 2
    c, s = jnp.where(first, table, turned), jnp.where(first, -turned, table)
    out = []
    for h in range(v.shape[1] // head):
        n = rms(v[:, h * head : (h + 1) * head], gain)
        out.append((n * c + pltpu.roll(n, head // 2, 1) * s).astype(BF16))
    return jnp.concatenate(out, axis=1)


def kv_kernel(*refs):
    srcs, (n_ref, kv_ref, k_ref, v_ref), bufs, sem = refs[:6], refs[6:10], refs[10:16], refs[16]
    copies = []
    for i, (src, buf) in enumerate(zip(srcs, bufs)):
        for j in range(2 if i < 4 else 1):
            part = src.shape[0] // 2 if i < 4 else 1
            at = pl.ds(j * part, part)
            copies.append(pltpu.make_async_copy(src.at[at], buf.at[at], sem.at[2 * i + j]))
    for copy in copies:
        copy.start()
    copies[8].wait()
    copies[9].wait()
    gain_ref, kg_ref = bufs[4:]
    x_ref, kw_ref, vw_ref, t_ref = bufs[:4]
    copies[0].wait()
    copies[1].wait()
    n = rms(x_ref[...].astype(F32), gain_ref[...]).astype(BF16)
    n_ref[...] = n
    width = kw_ref.shape[1]
    copies[2].wait()
    copies[3].wait()
    k = jnp.dot(n, kw_ref[...], preferred_element_type=F32)
    copies[6].wait()
    copies[7].wait()
    k = head_rope(k, kg_ref[...], t_ref[...])
    copies[4].wait()
    copies[5].wait()
    v = jnp.dot(n, vw_ref[...], preferred_element_type=F32).astype(BF16)
    k_ref[...] = k
    v_ref[...] = v
    kv_ref[:, :width] = k
    kv_ref[:, width:] = v


def q_kernel(n_ref, w_ref, g_ref, t_ref, q_ref):
    q = jnp.dot(n_ref[...], w_ref[...], preferred_element_type=F32)
    q_ref[...] = head_rope(q, g_ref[...], t_ref[...])


def attention_kernel(head, kv_heads, names, first, last, pos_ref, q_ref, *rest):
    rest = list(rest)
    carried = [] if first else [rest.pop(0) for _ in range(3)]
    blocks = [rest.pop(0) for _ in names]
    if last:
        out_ref = rest.pop(0)
    top, total, acc = rest
    rows = q_ref.shape[0]
    group = q_ref.shape[1] // (head * kv_heads)
    me = lax.axis_index("seq")
    scale = math.log2(math.e) / math.sqrt(head)
    query = me * rows + lax.broadcasted_iota(jnp.int32, (1, rows), 1)
    start = query - pos_ref[...]
    width = kv_heads * head

    def scores(g, ref, block):
        qs = [q_ref[:, (g * group + i) * head : (g * group + i + 1) * head] for i in range(group)]
        qg = jnp.concatenate(qs, axis=0)
        s = lax.dot_general(
            ref[:, g * head : (g + 1) * head], qg, (((1,), (1,)), ((), ())), preferred_element_type=F32
        )
        key = block * rows + lax.broadcasted_iota(jnp.int32, (rows, rows), 0)
        ok = (key >= start) & (key <= query)
        return jnp.where(jnp.concatenate([ok] * group, axis=1), s * scale, -1e30)

    def weigh(g, ref, p):
        return lax.dot_general(
            ref[:, width + g * head : width + (g + 1) * head],
            p.astype(BF16),
            (((0,), (0,)), ((), ())),
            preferred_element_type=F32,
        )

    for new, old in zip((top, total, acc), carried):
        new[...] = old[...]
    for i, ((name, swapped), ref) in enumerate(zip(names, blocks)):
        if first and i == 0:
            for g in range(kv_heads):
                s = scores(g, ref, me)
                m = jnp.max(s, axis=0, keepdims=True)
                p = jnp.exp2(s - m)
                top[g] = m
                total[g] = jnp.sum(p, axis=0, keepdims=True)
                acc[g] = weigh(g, ref, p)
            continue
        block = {"here": me, "pair": me - 2, "far": me - 4, "far pair": (me ^ 2) - 4}[name]
        there = (block >= 0) & ((me // 2) % 2 == 1 if name == "pair" else True)
        if swapped:
            block = block ^ 1

        @pl.when(there & (block < me))
        def _():
            for g in range(kv_heads):
                s = scores(g, ref, block)
                old = top[g]
                m = jnp.maximum(old, jnp.max(s, axis=0, keepdims=True))
                p = jnp.exp2(s - m)
                decay = jnp.exp2(old - m)
                top[g] = m
                total[g] = total[g] * decay + jnp.sum(p, axis=0, keepdims=True)
                acc[g] = acc[g] * decay + weigh(g, ref, p)

    if last:
        for g in range(kv_heads):
            a = (acc[g] / total[g]).T.astype(BF16)
            for i in range(group):
                h = g * group + i
                out_ref[:, h * head : (h + 1) * head] = a[i * rows : (i + 1) * rows]


def halves_kernel(gate_ref, up_ref, down_ref, *outs):
    rows, width = gate_ref.shape[0], outs[0].shape[1]
    keep = (lax.axis_index("seq") // 2) % 2
    for g_ref, d_ref, which in (outs[:2] + (keep,), outs[2:4] + (1 - keep,)):
        at = pl.ds(pl.multiple_of(which * width, 128), width)
        g_ref[:rows, :] = gate_ref[:, at]
        g_ref[rows:, :] = up_ref[:, at]
        d_ref[...] = down_ref[at, :].T
    outs[4][: 2 * rows, :] = outs[0][...]
    outs[4][2 * rows :, :] = outs[1][...]


def out_kernel(mine_ref, other_ref, w_mine_ref, w_other_ref, *outs):
    part = outs[0].shape[0]
    first = (lax.axis_index("tp") % 2) * 2 * part
    w = jnp.concatenate([w_mine_ref[...], w_other_ref[...]], axis=0)
    for i, out_ref in enumerate(outs):
        rows = pl.ds(pl.multiple_of(first + i * part, part), part)
        a = jnp.concatenate([mine_ref[rows, :], other_ref[rows, :]], axis=1)
        out_ref[...] = jnp.dot(a, w, preferred_element_type=F32).astype(BF16)


def mid_kernel(which, x_ref, a_ref, b_ref, mid_ref):
    part = mid_ref.shape[0]
    first = (lax.axis_index("tp") % 2) * 2 * part + which * part
    x = x_ref[pl.ds(pl.multiple_of(first, part), part), :]
    mid_ref[...] = (x.astype(F32) + (a_ref[...].astype(F32) + b_ref[...].astype(F32))).astype(BF16)


def act_kernel(*refs):
    blocks, gain_ref, pieces, (act_ref, n_ref) = refs[:8], refs[8], refs[9:17], refs[17:]
    part = blocks[0].shape[0]
    wide = pieces[2].shape[0] // 2
    me = lax.axis_index("seq")
    for i, ref in enumerate(blocks):
        n_ref[i * part : (i + 1) * part, :] = rms(ref[...].astype(F32), gain_ref[...]).astype(BF16)
    n = jnp.concatenate(
        [n_ref[:, pl.ds(pl.multiple_of((me ^ k) * wide, wide), wide)] for k in range(8)], axis=1
    )
    wg = jnp.concatenate([ref[:wide, :] for ref in pieces], axis=0)
    wu = jnp.concatenate([ref[wide : 2 * wide, :] for ref in pieces], axis=0)
    gate = jnp.dot(n, wg, preferred_element_type=F32)
    up = jnp.dot(n, wu, preferred_element_type=F32)
    act_ref[...] = (gate / (1.0 + jnp.exp(-gate)) * up).astype(BF16)


def down_kernel(shards, act_ref, *rest):
    pieces, (away_ref, keep_ref) = rest[:-2], rest[-2:]
    rows = act_ref.shape[0] // 2
    wide = keep_ref.shape[1] // len(pieces)
    for i, ref in enumerate(pieces):
        other = shards.index(shards[i] ^ 2)
        at = i + (lax.axis_index("seq") // 2) % 2 * (other - i)
        cols = pl.ds(pl.multiple_of(at * wide, wide), wide)
        w = ref[ref.shape[0] - wide :, :]
        t = lax.dot_general(act_ref[...], w, (((1,), (1,)), ((), ())), preferred_element_type=F32)
        keep_ref[:, cols] = t[:rows]
        away_ref[:, cols] = t[rows:].astype(BF16)


def split_sum_kernel(keep_ref, away_ref, own_ref, part_ref):
    half = own_ref.shape[0]
    own_ref[...] = (keep_ref[:half, :].astype(F32) + away_ref[:half, :].astype(F32)).astype(BF16)
    part_ref[...] = (keep_ref[half:, :].astype(F32) + away_ref[half:, :].astype(F32)).astype(BF16)


def sum_kernel(a_ref, b_ref, out_ref):
    out_ref[...] = (a_ref[...].astype(F32) + b_ref[...].astype(F32)).astype(BF16)


def last_sum_kernel(shards, mid_a_ref, mid_b_ref, a_ref, b_ref, out_ref):
    wide = out_ref.shape[1] // len(shards)
    me = lax.axis_index("seq") & 5
    for i, k in enumerate(shards):
        here = slice(i * wide, (i + 1) * wide)
        cols = pl.ds(pl.multiple_of((me ^ k) * wide, wide), wide)
        mid = jnp.concatenate([mid_a_ref[:, cols], mid_b_ref[:, cols]], axis=0).astype(F32)
        add = a_ref[:, here].astype(F32) + b_ref[:, here].astype(F32)
        out_ref[:, here] = (mid + add).astype(BF16)


def place_kernel(parts, *rest):
    pairs, out_ref = rest[:-1], rest[-1]
    core = lax.axis_index("tp") % 2
    me = lax.axis_index("seq") & 5
    for shards, keep_ref, away_ref in zip(parts, pairs[0::2], pairs[1::2]):
        half = keep_ref.shape[0]
        wide = keep_ref.shape[1] // len(shards)
        for i, k in enumerate(shards):
            cols = pl.ds(pl.multiple_of((me ^ k) * wide, wide), wide)
            here = slice(i * wide, (i + 1) * wide)
            out_ref[pl.ds(pl.multiple_of(core * half, half), half), cols] = keep_ref[:, here]
            out_ref[pl.ds(pl.multiple_of((1 - core) * half, half), half), cols] = away_ref[:, here]


def grid_body(
    layer_input, norm_gain, w_query, key_weight, value_weight, w_out, query_gain, key_gain,
    seg_ids, positions, post_gain, w_gate, w_up, w_down,
):
    rows, model = layer_input.shape
    head = query_gain.shape[0]
    kv_heads = key_weight.shape[1] // head
    kv_width = key_weight.shape[1]
    me = lax.axis_index("seq")
    core = lax.axis_index("tp") % 2
    half = rows // 2
    ff = w_gate.shape[1] // 2
    sds = jax.ShapeDtypeStruct

    def send(name, v, axis, pairs):
        with jax.named_scope(name):
            return lax.ppermute(v, axis, pairs)

    def swap(name, v, mask, who=range(8)):
        return send(name, v, "seq", [(a, a ^ mask) for a in who])

    def later(name, v, z, who=range(4)):
        return send(name, v, "seq", [(a, a + 2 * z) for a in who])

    def swap_tp(name, v, mask):
        return send(name, v, "tp", [(t, t ^ mask) for t in range(4)])

    tie = lax.optimization_barrier
    reached = []

    def step(value):
        now = len(reached)
        here = [name for name in PLAN if PLAN[name][1] == now]
        value, there = tie((value, [get(name) for name in here]))
        sent.update(zip(here, there))
        reached.append(value)
        return value

    def get(name):
        if name not in sent:
            operand, send_one = transfers[name]
            operand = get(operand) if isinstance(operand, str) else operand
            after = PLAN[name][0]
            if after is not None:
                operand = tie((operand, reached[after]))[0]
            sent[name] = send_one(name, operand)
        return sent[name]

    sent = {}
    w_c = swap_tp("w_c", w_out, 1)
    table = rope_table(positions, head)
    normed, kv, key_cache, value_cache = call(
        kv_kernel,
        [sds((rows, model), BF16), sds((rows, 2 * kv_width), BF16)] + [sds((rows, kv_width), BF16)] * 2,
        layer_input, key_weight, value_weight, table, norm_gain[None], key_gain[None],
        scratch=[pltpu.VMEM(v.shape, v.dtype) for v in (layer_input, key_weight, value_weight, table)]
        + [pltpu.VMEM((1, v.shape[0]), F32) for v in (norm_gain, key_gain)]
        + [pltpu.SemaphoreType.DMA((12,))],
        hbm=6,
        vmem=KV_VMEM_BYTES,
    )
    w_late, w_c = tie((w_gate, kv, w_c))[::2]
    shapes = [sds((n * w_gate.shape[0], ff), BF16) for n in (2, 1, 3)]
    g_mine, d_mine, g_theirs, d_theirs, w_mine = call(
        halves_kernel, shapes[:2] * 2 + shapes[2:], w_late, w_up, w_down
    )
    q = call(
        q_kernel, sds((rows, w_query.shape[1]), BF16), normed, w_query, query_gain[None], table,
    )

    def along(mask, who=range(8)):
        return lambda name, v: swap(name, v, mask, who)

    transfers = {
        "k1": (kv, lambda name, v: later(name, v, 1, (0, 1, 4, 5))),
        "k0x": (kv, along(1, (0, 2, 4, 6))),
        "k1x": ("k1", along(1, (2, 3, 6, 7))),
        "k2x": ("k2", along(1, (4, 5, 6, 7))),
        "w1": (w_mine, along(1)),
        "g2": (g_theirs, along(2)),
        "g4": (g_mine, along(4)),
        "g6": (g_theirs, along(6)),
        "d2": (d_theirs, along(2)),
        "d4": (d_mine, along(4)),
        "d6": (d_theirs, along(6)),
        "g2x": ("g2", along(1)),
        "g4x": ("g4", along(1)),
        "g6x": ("g6", along(1)),
        "d2x": ("d2", along(1)),
        "d4x": ("d4", along(1)),
        "d6x": ("d6", along(1)),
    }
    kv_out = step(kv)
    k2 = later("k2", kv_out, 2)
    k2, q = tie((k2, q))
    k2 = sent["k2"] = step(k2)
    k3 = step(swap("k3", k2, 2, (4, 5, 6, 7)))
    group_rows = rows * (w_query.shape[1] // kv_width)
    state = [sds((kv_heads, 1, group_rows), F32)] * 2 + [sds((kv_heads, head, group_rows), F32)]
    attend = functools.partial(attention_kernel, head, kv_heads)
    early = [("here", False), ("pair", False), ("pair", True)]
    early += [("far", False), ("far", True), ("far pair", False)]
    k3x = swap("k3x", k3, 1, (4, 5, 6, 7))
    state = call(
        functools.partial(attend, early, True, False), state,
        positions[None], q, kv, get("k1"), get("k1x"), k2, get("k2x"), k3,
    )
    state = step(state)
    k3x = step(k3x)
    a0 = call(
        functools.partial(attend, [("here", True), ("far pair", True)], False, True),
        sds((rows, w_query.shape[1]), BF16),
        positions[None], q, *state, get("k0x"), k3x,
        scratch=[pltpu.VMEM(v.shape, F32) for v in state],
    )
    a0 = step(a0)
    quarter = sds((half // 2, model), BF16)
    outs = step(call(out_kernel, [quarter] * 2, a0, swap_tp("ac", a0, 1), w_out, w_c))
    out_ya, out_yb = swap_tp("out y a", outs[0], 2), swap_tp("out y b", outs[1], 2)
    out_ya = step(out_ya)
    mid_a = call(functools.partial(mid_kernel, 0), quarter, layer_input, outs[0], out_ya)
    part_a = swap("mid z a", mid_a, 2)
    mid_b = step(call(functools.partial(mid_kernel, 1), quarter, layer_input, outs[1], out_yb))
    part_b = step(swap("mid z b", mid_b, 2))
    rows_here = [mid_a, mid_b, part_a, part_b]
    rows_away = [swap_tp("rows core", v, 1) for v in rows_here]
    act = call(
        act_kernel, sds((2 * rows, ff), BF16),
        *rows_here, *rows_away, post_gain[None],
        g_mine, get("w1"), *[get(name) for name in ("g2", "g2x", "g4", "g4x", "g6", "g6x")],
        scratch=[pltpu.VMEM((2 * rows, model), BF16)],
    )
    act = step(act)
    wide = w_down.shape[1]
    downs = [d_mine, get("w1")] + [get(n) for n in ("d2", "d2x", "d4", "d4x", "d6", "d6x")]

    def down(shards, act):
        cols = len(shards) * wide
        away, own = call(
            functools.partial(down_kernel, shards), [sds((rows, cols), BF16), sds((rows, cols), F32)],
            act, *[downs[k] for k in shards],
        )
        return own, swap_tp("sum core", away, 1)

    def last(shards, a, b):
        done = call(
            functools.partial(last_sum_kernel, shards), sds((half, len(shards) * wide), BF16), mid_a, mid_b, a, b
        )
        return [done, swap_tp("rows", done, 1)]

    def over_z(shards, act):
        own, away = down(shards, act)
        mine, theirs = call(split_sum_kernel, [sds((half, len(shards) * wide), BF16)] * 2, own, away)
        return call(sum_kernel, sds(mine.shape, BF16), mine, swap("sum z", theirs, 2))

    chip = over_z(FIRST, act)
    act, chip = tie((act, chip))
    pairs = last(FIRST, chip, swap_tp("sum y", chip, 2))
    chip = over_z(OTHER, act)
    pairs += last(OTHER, chip, swap_tp("sum y", chip, 2))
    hidden = call(functools.partial(place_kernel, (FIRST, OTHER)), sds((rows, model), BF16), *pairs)
    return (hidden, key_cache, value_cache)


def rope(v, place):
    half = v.shape[-1] // 2
    table = rope_table(place, v.shape[-1])[:, None, :]
    c, s = table[..., :half], table[..., half:]
    a, b = v[..., :half], v[..., half:]
    return jnp.concatenate([a * c - b * s, b * c + a * s], axis=-1)


def general_body(
    layer_input, norm_gain, w_query, key_weight, value_weight, w_out, query_gain, key_gain,
    seg_ids, positions, post_gain, w_gate, w_up, w_down,
):
    rows = layer_input.shape[0]
    head = query_gain.shape[0]
    kv_local = key_weight.shape[1] // head
    group = w_query.shape[1] // head // kv_local
    scale = 1.0 / math.sqrt(head)
    xf = layer_input.astype(F32)
    normed = rms(xf, norm_gain).astype(BF16)

    def heads(w, gain):
        v = jnp.dot(normed, w, preferred_element_type=F32).reshape(rows, -1, head)
        return rope(rms(v, gain), positions).astype(BF16)

    q = heads(w_query, query_gain).reshape(rows, kv_local, group, head).transpose(1, 2, 0, 3)
    key_cache = heads(key_weight, key_gain).reshape(rows, kv_local * head)
    value_cache = jnp.dot(normed, value_weight, preferred_element_type=F32).astype(BF16)
    me = lax.axis_index("seq")
    keys = lax.all_gather(key_cache, "seq", axis=0, tiled=True)
    values = lax.all_gather(value_cache, "seq", axis=0, tiled=True)
    query = me * rows + jnp.arange(rows, dtype=jnp.int32)
    start = query - positions
    width = rows * math.gcd(keys.shape[0] // rows, max(1, 1024 // rows))

    def update(state, kb, vb, offset):
        top, total, acc = state
        kb = kb.reshape(width, kv_local, head)
        s = jnp.einsum("hgqd,khd->hgqk", q, kb, preferred_element_type=F32) * scale
        key = offset + jnp.arange(width, dtype=jnp.int32)
        ok = (key[None, :] >= start[:, None]) & (key[None, :] <= query[:, None])
        s = jnp.where(ok, s, -1e30)
        new_top = jnp.maximum(top, jnp.max(s, axis=-1))
        p = jnp.where(ok, jnp.exp(s - new_top[..., None]), 0.0)
        decay = jnp.exp(top - new_top)
        vb = vb.reshape(width, kv_local, head)
        add = jnp.einsum("hgqk,khd->hgqd", p.astype(BF16), vb, preferred_element_type=F32)
        return (new_top, total * decay + jnp.sum(p, axis=-1), acc * decay[..., None] + add)

    def one_block(step, state):
        offset = step * width
        kb = lax.dynamic_slice_in_dim(keys, offset, width, 0)
        vb = lax.dynamic_slice_in_dim(values, offset, width, 0)
        skip = (offset > query[-1]) | (offset + width <= start[0])
        return lax.cond(skip, lambda c: c, lambda c: update(c, kb, vb, offset), state)

    state = (
        jnp.full((kv_local, group, rows), -1e30, F32),
        jnp.zeros((kv_local, group, rows), F32),
        jnp.zeros((kv_local, group, rows, head), F32),
    )
    top, total, acc = lax.fori_loop(0, keys.shape[0] // width, one_block, state)
    attended = (acc / total[..., None]).astype(BF16).transpose(2, 0, 1, 3).reshape(rows, -1)
    partial_out = jnp.dot(attended, w_out, preferred_element_type=F32)
    summed = lax.psum(partial_out.astype(BF16), "tp").astype(F32)
    mid = (xf + summed).astype(BF16)
    mid_f = mid.astype(F32)
    post_normed = rms(mid_f, post_gain).astype(BF16)
    gate_w = lax.all_gather(w_gate, "seq", axis=0, tiled=True)
    up_w = lax.all_gather(w_up, "seq", axis=0, tiled=True)
    down_w = lax.all_gather(w_down, "seq", axis=1, tiled=True)
    gate = jnp.dot(post_normed, gate_w, preferred_element_type=F32)
    up = jnp.dot(post_normed, up_w, preferred_element_type=F32)
    act = (jax.nn.silu(gate) * up).astype(BF16)
    terms = jnp.dot(act, down_w, preferred_element_type=F32)
    ffn_total = lax.psum(terms.astype(BF16), "tp").astype(F32)
    hidden = (mid_f + ffn_total).astype(BF16)
    return (hidden, key_cache, value_cache)


def solution(mesh):
    in_specs = (
        P("seq", None),
        P(),
        P(None, "tp"),
        P(None, "tp"),
        P(None, "tp"),
        P("tp", None),
        P(),
        P(),
        P("seq"),
        P("seq"),
        P(),
        P("seq", "tp"),
        P("seq", "tp"),
        P("tp", "seq"),
    )
    out_specs = (P("seq", None), P("seq", "tp"), P("seq", "tp"))
    body = grid_body if (mesh.shape["seq"], mesh.shape["tp"]) == (8, 4) else general_body
    return jax.shard_map(body, mesh=mesh, in_specs=in_specs, out_specs=out_specs, check_vma=False)
```

```python
import functools
import math

import jax
import jax.numpy as jnp
from jax import lax
from jax.experimental import pallas as pl
from jax.experimental.pallas import tpu as pltpu
from jax.sharding import PartitionSpec as P

F32 = jnp.float32
BF16 = jnp.bfloat16
EPS = 1e-06
VMEM_BYTES = 16 * 1024 * 1024
KV_VMEM_BYTES = 59 * 1024 * 1024
FIRST, OTHER = (0, 1, 2, 3, 4, 6), (5, 7)
PLAN = {'k1': (0, None),
 'k0x': (0, 2),
 'k1x': (None, None),
 'k2x': (None, None),
 'w1': (0, 4),
 'g6': (None, None),
 'g2': (2, 8),
 'g4': (2, None),
 'g6x': (7, None),
 'g2x': (None, 7),
 'g4x': (1, None),
 'd6': (5, 10),
 'd4': (6, 9),
 'd2': (7, None),
 'd6x': (None, None),
 'd4x': (1, None),
 'd2x': (None, None)}

def rms(v, gain):
    return v * lax.rsqrt(jnp.mean(v * v, axis=-1, keepdims=True) + EPS) * gain


def rope_table(positions, head):
    half = head // 2
    freqs = 1000000.0 ** (-2.0 * jnp.arange(half, dtype=F32) / head)
    angle = positions.astype(F32)[:, None] * freqs[None, :]
    return jnp.concatenate([jnp.cos(angle), jnp.sin(angle)], axis=-1)


def call(kernel, out_shape, *args, scratch=(), hbm=0, vmem=VMEM_BYTES):
    vm = pl.BlockSpec(memory_space=pltpu.VMEM)
    many = isinstance(out_shape, (list, tuple))
    return pl.pallas_call(
        kernel,
        out_shape=out_shape,
        in_specs=[pl.BlockSpec(memory_space=pltpu.HBM)] * hbm + [vm] * (len(args) - hbm),
        out_specs=[vm] * len(out_shape) if many else vm,
        scratch_shapes=list(scratch),
        compiler_params=pltpu.CompilerParams(vmem_limit_bytes=vmem),
        cost_estimate=pl.CostEstimate(flops=1, bytes_accessed=1, transcendentals=0),
    )(*args)


def head_rope(v, gain, table):
    head = gain.shape[-1]
    turned = pltpu.roll(table, head // 2, 1)
    first = lax.broadcasted_iota(jnp.int32, table.shape, 1) < head // 2
    c, s = jnp.where(first, table, turned), jnp.where(first, -turned, table)
    out = []
    for h in range(v.shape[1] // head):
        n = rms(v[:, h * head : (h + 1) * head], gain)
        out.append((n * c + pltpu.roll(n, head // 2, 1) * s).astype(BF16))
    return jnp.concatenate(out, axis=1)


def kv_kernel(*refs):
    srcs, (n_ref, kv_ref, k_ref, v_ref), bufs, sem = refs[:6], refs[6:10], refs[10:16], refs[16]
    copies = []
    for i, (src, buf) in enumerate(zip(srcs, bufs)):
        for j in range(2 if i < 4 else 1):
            part = src.shape[0] // 2 if i < 4 else 1
            at = pl.ds(j * part, part)
            copies.append(pltpu.make_async_copy(src.at[at], buf.at[at], sem.at[2 * i + j]))
    for copy in copies:
        copy.start()
    copies[8].wait()
    copies[9].wait()
    gain_ref, kg_ref = bufs[4:]
    x_ref, kw_ref, vw_ref, t_ref = bufs[:4]
    copies[0].wait()
    copies[1].wait()
    n = rms(x_ref[...].astype(F32), gain_ref[...]).astype(BF16)
    n_ref[...] = n
    width = kw_ref.shape[1]
    copies[2].wait()
    copies[3].wait()
    k = jnp.dot(n, kw_ref[...], preferred_element_type=F32)
    copies[6].wait()
    copies[7].wait()
    k = head_rope(k, kg_ref[...], t_ref[...])
    copies[4].wait()
    copies[5].wait()
    v = jnp.dot(n, vw_ref[...], preferred_element_type=F32).astype(BF16)
    k_ref[...] = k
    v_ref[...] = v
    kv_ref[:, :width] = k
    kv_ref[:, width:] = v


def q_kernel(n_ref, w_ref, g_ref, t_ref, q_ref):
    q = jnp.dot(n_ref[...], w_ref[...], preferred_element_type=F32)
    q_ref[...] = head_rope(q, g_ref[...], t_ref[...])


def attention_kernel(head, kv_heads, names, first, last, pos_ref, q_ref, *rest):
    rest = list(rest)
    carried = [] if first else [rest.pop(0) for _ in range(3)]
    blocks = [rest.pop(0) for _ in names]
    if last:
        out_ref = rest.pop(0)
    top, total, acc = rest
    rows = q_ref.shape[0]
    group = q_ref.shape[1] // (head * kv_heads)
    me = lax.axis_index("seq")
    scale = math.log2(math.e) / math.sqrt(head)
    query = me * rows + lax.broadcasted_iota(jnp.int32, (1, rows), 1)
    start = query - pos_ref[...]
    width = kv_heads * head

    def scores(g, ref, block):
        qs = [q_ref[:, (g * group + i) * head : (g * group + i + 1) * head] for i in range(group)]
        qg = jnp.concatenate(qs, axis=0)
        s = lax.dot_general(
            ref[:, g * head : (g + 1) * head], qg, (((1,), (1,)), ((), ())), preferred_element_type=F32
        )
        key = block * rows + lax.broadcasted_iota(jnp.int32, (rows, rows), 0)
        ok = (key >= start) & (key <= query)
        return jnp.where(jnp.concatenate([ok] * group, axis=1), s * scale, -1e30)

    def weigh(g, ref, p):
        return lax.dot_general(
            ref[:, width + g * head : width + (g + 1) * head],
            p.astype(BF16),
            (((0,), (0,)), ((), ())),
            preferred_element_type=F32,
        )

    for new, old in zip((top, total, acc), carried):
        new[...] = old[...]
    for i, ((name, swapped), ref) in enumerate(zip(names, blocks)):
        if first and i == 0:
            for g in range(kv_heads):
                s = scores(g, ref, me)
                m = jnp.max(s, axis=0, keepdims=True)
                p = jnp.exp2(s - m)
                top[g] = m
                total[g] = jnp.sum(p, axis=0, keepdims=True)
                acc[g] = weigh(g, ref, p)
            continue
        block = {"here": me, "pair": me - 2, "far": me - 4, "far pair": (me ^ 2) - 4}[name]
        there = (block >= 0) & ((me // 2) % 2 == 1 if name == "pair" else True)
        if swapped:
            block = block ^ 1

        @pl.when(there & (block < me))
        def _():
            for g in range(kv_heads):
                s = scores(g, ref, block)
                old = top[g]
                m = jnp.maximum(old, jnp.max(s, axis=0, keepdims=True))
                p = jnp.exp2(s - m)
                decay = jnp.exp2(old - m)
                top[g] = m
                total[g] = total[g] * decay + jnp.sum(p, axis=0, keepdims=True)
                acc[g] = acc[g] * decay + weigh(g, ref, p)

    if last:
        for g in range(kv_heads):
            a = (acc[g] / total[g]).T.astype(BF16)
            for i in range(group):
                h = g * group + i
                out_ref[:, h * head : (h + 1) * head] = a[i * rows : (i + 1) * rows]


def halves_kernel(gate_ref, up_ref, down_ref, *outs):
    rows, width = gate_ref.shape[0], outs[0].shape[1]
    keep = (lax.axis_index("seq") // 2) % 2
    for g_ref, d_ref, which in (outs[:2] + (keep,), outs[2:4] + (1 - keep,)):
        at = pl.ds(pl.multiple_of(which * width, 128), width)
        g_ref[:rows, :] = gate_ref[:, at]
        g_ref[rows:, :] = up_ref[:, at]
        d_ref[...] = down_ref[at, :].T
    outs[4][: 2 * rows, :] = outs[0][...]
    outs[4][2 * rows :, :] = outs[1][...]


def out_kernel(mine_ref, other_ref, w_mine_ref, w_other_ref, *outs):
    part = outs[0].shape[0]
    first = (lax.axis_index("tp") % 2) * 2 * part
    w = jnp.concatenate([w_mine_ref[...], w_other_ref[...]], axis=0)
    for i, out_ref in enumerate(outs):
        rows = pl.ds(pl.multiple_of(first + i * part, part), part)
        a = jnp.concatenate([mine_ref[rows, :], other_ref[rows, :]], axis=1)
        out_ref[...] = jnp.dot(a, w, preferred_element_type=F32).astype(BF16)


def mid_kernel(which, x_ref, a_ref, b_ref, mid_ref):
    part = mid_ref.shape[0]
    first = (lax.axis_index("tp") % 2) * 2 * part + which * part
    x = x_ref[pl.ds(pl.multiple_of(first, part), part), :]
    mid_ref[...] = (x.astype(F32) + (a_ref[...].astype(F32) + b_ref[...].astype(F32))).astype(BF16)


def act_kernel(*refs):
    blocks, gain_ref, pieces, (act_ref, n_ref) = refs[:8], refs[8], refs[9:17], refs[17:]
    part = blocks[0].shape[0]
    wide = pieces[2].shape[0] // 2
    me = lax.axis_index("seq")
    for i, ref in enumerate(blocks):
        n_ref[i * part : (i + 1) * part, :] = rms(ref[...].astype(F32), gain_ref[...]).astype(BF16)
    n = jnp.concatenate(
        [n_ref[:, pl.ds(pl.multiple_of((me ^ k) * wide, wide), wide)] for k in range(8)], axis=1
    )
    wg = jnp.concatenate([ref[:wide, :] for ref in pieces], axis=0)
    wu = jnp.concatenate([ref[wide : 2 * wide, :] for ref in pieces], axis=0)
    gate = jnp.dot(n, wg, preferred_element_type=F32)
    up = jnp.dot(n, wu, preferred_element_type=F32)
    act_ref[...] = (gate / (1.0 + jnp.exp(-gate)) * up).astype(BF16)


def down_kernel(shards, act_ref, *rest):
    pieces, (away_ref, keep_ref) = rest[:-2], rest[-2:]
    rows = act_ref.shape[0] // 2
    wide = keep_ref.shape[1] // len(pieces)
    for i, ref in enumerate(pieces):
        other = shards.index(shards[i] ^ 2)
        at = i + (lax.axis_index("seq") // 2) % 2 * (other - i)
        cols = pl.ds(pl.multiple_of(at * wide, wide), wide)
        w = ref[ref.shape[0] - wide :, :]
        t = lax.dot_general(act_ref[...], w, (((1,), (1,)), ((), ())), preferred_element_type=F32)
        keep_ref[:, cols] = t[:rows]
        away_ref[:, cols] = t[rows:].astype(BF16)


def split_sum_kernel(keep_ref, away_ref, own_ref, part_ref):
    half = own_ref.shape[0]
    own_ref[...] = (keep_ref[:half, :].astype(F32) + away_ref[:half, :].astype(F32)).astype(BF16)
    part_ref[...] = (keep_ref[half:, :].astype(F32) + away_ref[half:, :].astype(F32)).astype(BF16)


def sum_kernel(a_ref, b_ref, out_ref):
    out_ref[...] = (a_ref[...].astype(F32) + b_ref[...].astype(F32)).astype(BF16)


def last_sum_kernel(shards, mid_a_ref, mid_b_ref, a_ref, b_ref, out_ref):
    wide = out_ref.shape[1] // len(shards)
    me = lax.axis_index("seq") & 5
    for i, k in enumerate(shards):
        here = slice(i * wide, (i + 1) * wide)
        cols = pl.ds(pl.multiple_of((me ^ k) * wide, wide), wide)
        mid = jnp.concatenate([mid_a_ref[:, cols], mid_b_ref[:, cols]], axis=0).astype(F32)
        add = a_ref[:, here].astype(F32) + b_ref[:, here].astype(F32)
        out_ref[:, here] = (mid + add).astype(BF16)


def place_kernel(parts, *rest):
    pairs, out_ref = rest[:-1], rest[-1]
    core = lax.axis_index("tp") % 2
    me = lax.axis_index("seq") & 5
    for shards, keep_ref, away_ref in zip(parts, pairs[0::2], pairs[1::2]):
        half = keep_ref.shape[0]
        wide = keep_ref.shape[1] // len(shards)
        for i, k in enumerate(shards):
            cols = pl.ds(pl.multiple_of((me ^ k) * wide, wide), wide)
            here = slice(i * wide, (i + 1) * wide)
            out_ref[pl.ds(pl.multiple_of(core * half, half), half), cols] = keep_ref[:, here]
            out_ref[pl.ds(pl.multiple_of((1 - core) * half, half), half), cols] = away_ref[:, here]


def grid_body(
    layer_input, norm_gain, w_query, key_weight, value_weight, w_out, query_gain, key_gain,
    seg_ids, positions, post_gain, w_gate, w_up, w_down,
):
    rows, model = layer_input.shape
    head = query_gain.shape[0]
    kv_heads = key_weight.shape[1] // head
    kv_width = key_weight.shape[1]
    me = lax.axis_index("seq")
    core = lax.axis_index("tp") % 2
    half = rows // 2
    ff = w_gate.shape[1] // 2
    sds = jax.ShapeDtypeStruct

    def send(name, v, axis, pairs):
        with jax.named_scope(name):
            return lax.ppermute(v, axis, pairs)

    def swap(name, v, mask, who=range(8)):
        return send(name, v, "seq", [(a, a ^ mask) for a in who])

    def later(name, v, z, who=range(4)):
        return send(name, v, "seq", [(a, a + 2 * z) for a in who])

    def swap_tp(name, v, mask):
        return send(name, v, "tp", [(t, t ^ mask) for t in range(4)])

    tie = lax.optimization_barrier
    reached = []

    def step(value):
        now = len(reached)
        here = [name for name in PLAN if PLAN[name][1] == now]
        value, there = tie((value, [get(name) for name in here]))
        sent.update(zip(here, there))
        reached.append(value)
        return value

    def get(name):
        if name not in sent:
            operand, send_one = transfers[name]
            operand = get(operand) if isinstance(operand, str) else operand
            after = PLAN[name][0]
            if after is not None:
                operand = tie((operand, reached[after]))[0]
            sent[name] = send_one(name, operand)
        return sent[name]

    sent = {}
    w_c = swap_tp("w_c", w_out, 1)
    table = rope_table(positions, head)
    normed, kv, key_cache, value_cache = call(
        kv_kernel,
        [sds((rows, model), BF16), sds((rows, 2 * kv_width), BF16)] + [sds((rows, kv_width), BF16)] * 2,
        layer_input, key_weight, value_weight, table, norm_gain[None], key_gain[None],
        scratch=[pltpu.VMEM(v.shape, v.dtype) for v in (layer_input, key_weight, value_weight, table)]
        + [pltpu.VMEM((1, v.shape[0]), F32) for v in (norm_gain, key_gain)]
        + [pltpu.SemaphoreType.DMA((12,))],
        hbm=6,
        vmem=KV_VMEM_BYTES,
    )
    w_late, w_c = tie((w_gate, kv, w_c))[::2]
    shapes = [sds((n * w_gate.shape[0], ff), BF16) for n in (2, 1, 3)]
    g_mine, d_mine, g_theirs, d_theirs, w_mine = call(
        halves_kernel, shapes[:2] * 2 + shapes[2:], w_late, w_up, w_down
    )
    q = call(
        q_kernel, sds((rows, w_query.shape[1]), BF16), normed, w_query, query_gain[None], table,
    )

    def along(mask, who=range(8)):
        return lambda name, v: swap(name, v, mask, who)

    transfers = {
        "k1": (kv, lambda name, v: later(name, v, 1, (0, 1, 4, 5))),
        "k0x": (kv, along(1, (0, 2, 4, 6))),
        "k1x": ("k1", along(1, (2, 3, 6, 7))),
        "k2x": ("k2", along(1, (4, 5, 6, 7))),
        "w1": (w_mine, along(1)),
        "g2": (g_theirs, along(2)),
        "g4": (g_mine, along(4)),
        "g6": (g_theirs, along(6)),
        "d2": (d_theirs, along(2)),
        "d4": (d_mine, along(4)),
        "d6": (d_theirs, along(6)),
        "g2x": ("g2", along(1)),
        "g4x": ("g4", along(1)),
        "g6x": ("g6", along(1)),
        "d2x": ("d2", along(1)),
        "d4x": ("d4", along(1)),
        "d6x": ("d6", along(1)),
    }
    kv_out = step(kv)
    k2 = later("k2", kv_out, 2)
    k2, q = tie((k2, q))
    k2 = sent["k2"] = step(k2)
    k3 = step(swap("k3", k2, 2, (4, 5, 6, 7)))
    group_rows = rows * (w_query.shape[1] // kv_width)
    state = [sds((kv_heads, 1, group_rows), F32)] * 2 + [sds((kv_heads, head, group_rows), F32)]
    attend = functools.partial(attention_kernel, head, kv_heads)
    early = [("here", False), ("pair", False), ("pair", True)]
    early += [("far", False), ("far", True), ("far pair", False)]
    k3x = swap("k3x", k3, 1, (4, 5, 6, 7))
    state = call(
        functools.partial(attend, early, True, False), state,
        positions[None], q, kv, get("k1"), get("k1x"), k2, get("k2x"), k3,
    )
    state = step(state)
    k3x = step(k3x)
    a0 = call(
        functools.partial(attend, [("here", True), ("far pair", True)], False, True),
        sds((rows, w_query.shape[1]), BF16),
        positions[None], q, *state, get("k0x"), k3x,
        scratch=[pltpu.VMEM(v.shape, F32) for v in state],
    )
    a0 = step(a0)
    quarter = sds((half // 2, model), BF16)
    outs = step(call(out_kernel, [quarter] * 2, a0, swap_tp("ac", a0, 1), w_out, w_c))
    out_ya, out_yb = swap_tp("out y a", outs[0], 2), swap_tp("out y b", outs[1], 2)
    out_ya = step(out_ya)
    mid_a = call(functools.partial(mid_kernel, 0), quarter, layer_input, outs[0], out_ya)
    part_a = swap("mid z a", mid_a, 2)
    mid_b = step(call(functools.partial(mid_kernel, 1), quarter, layer_input, outs[1], out_yb))
    part_b = step(swap("mid z b", mid_b, 2))
    rows_here = [mid_a, mid_b, part_a, part_b]
    rows_away = [swap_tp("rows core", v, 1) for v in rows_here]
    act = call(
        act_kernel, sds((2 * rows, ff), BF16),
        *rows_here, *rows_away, post_gain[None],
        g_mine, get("w1"), *[get(name) for name in ("g2", "g2x", "g4", "g4x", "g6", "g6x")],
        scratch=[pltpu.VMEM((2 * rows, model), BF16)],
    )
    act = step(act)
    wide = w_down.shape[1]
    downs = [d_mine, get("w1")] + [get(n) for n in ("d2", "d2x", "d4", "d4x", "d6", "d6x")]

    def down(shards, act):
        cols = len(shards) * wide
        away, own = call(
            functools.partial(down_kernel, shards), [sds((rows, cols), BF16), sds((rows, cols), F32)],
            act, *[downs[k] for k in shards],
        )
        return own, swap_tp("sum core", away, 1)

    def last(shards, a, b):
        done = call(
            functools.partial(last_sum_kernel, shards), sds((half, len(shards) * wide), BF16), mid_a, mid_b, a, b
        )
        return [done, swap_tp("rows", done, 1)]

    def over_z(shards, act):
        own, away = down(shards, act)
        mine, theirs = call(split_sum_kernel, [sds((half, len(shards) * wide), BF16)] * 2, own, away)
        return call(sum_kernel, sds(mine.shape, BF16), mine, swap("sum z", theirs, 2))

    chip = over_z(FIRST, act)

    pairs = last(FIRST, chip, swap_tp("sum y", chip, 2))
    chip = over_z(OTHER, act)
    pairs += last(OTHER, chip, swap_tp("sum y", chip, 2))
    hidden = call(functools.partial(place_kernel, (FIRST, OTHER)), sds((rows, model), BF16), *pairs)
    return (hidden, key_cache, value_cache)


def rope(v, place):
    half = v.shape[-1] // 2
    table = rope_table(place, v.shape[-1])[:, None, :]
    c, s = table[..., :half], table[..., half:]
    a, b = v[..., :half], v[..., half:]
    return jnp.concatenate([a * c - b * s, b * c + a * s], axis=-1)


def general_body(
    layer_input, norm_gain, w_query, key_weight, value_weight, w_out, query_gain, key_gain,
    seg_ids, positions, post_gain, w_gate, w_up, w_down,
):
    rows = layer_input.shape[0]
    head = query_gain.shape[0]
    kv_local = key_weight.shape[1] // head
    group = w_query.shape[1] // head // kv_local
    scale = 1.0 / math.sqrt(head)
    xf = layer_input.astype(F32)
    normed = rms(xf, norm_gain).astype(BF16)

    def heads(w, gain):
        v = jnp.dot(normed, w, preferred_element_type=F32).reshape(rows, -1, head)
        return rope(rms(v, gain), positions).astype(BF16)

    q = heads(w_query, query_gain).reshape(rows, kv_local, group, head).transpose(1, 2, 0, 3)
    key_cache = heads(key_weight, key_gain).reshape(rows, kv_local * head)
    value_cache = jnp.dot(normed, value_weight, preferred_element_type=F32).astype(BF16)
    me = lax.axis_index("seq")
    keys = lax.all_gather(key_cache, "seq", axis=0, tiled=True)
    values = lax.all_gather(value_cache, "seq", axis=0, tiled=True)
    query = me * rows + jnp.arange(rows, dtype=jnp.int32)
    start = query - positions
    width = rows * math.gcd(keys.shape[0] // rows, max(1, 1024 // rows))

    def update(state, kb, vb, offset):
        top, total, acc = state
        kb = kb.reshape(width, kv_local, head)
        s = jnp.einsum("hgqd,khd->hgqk", q, kb, preferred_element_type=F32) * scale
        key = offset + jnp.arange(width, dtype=jnp.int32)
        ok = (key[None, :] >= start[:, None]) & (key[None, :] <= query[:, None])
        s = jnp.where(ok, s, -1e30)
        new_top = jnp.maximum(top, jnp.max(s, axis=-1))
        p = jnp.where(ok, jnp.exp(s - new_top[..., None]), 0.0)
        decay = jnp.exp(top - new_top)
        vb = vb.reshape(width, kv_local, head)
        add = jnp.einsum("hgqk,khd->hgqd", p.astype(BF16), vb, preferred_element_type=F32)
        return (new_top, total * decay + jnp.sum(p, axis=-1), acc * decay[..., None] + add)

    def one_block(step, state):
        offset = step * width
        kb = lax.dynamic_slice_in_dim(keys, offset, width, 0)
        vb = lax.dynamic_slice_in_dim(values, offset, width, 0)
        skip = (offset > query[-1]) | (offset + width <= start[0])
        return lax.cond(skip, lambda c: c, lambda c: update(c, kb, vb, offset), state)

    state = (
        jnp.full((kv_local, group, rows), -1e30, F32),
        jnp.zeros((kv_local, group, rows), F32),
        jnp.zeros((kv_local, group, rows, head), F32),
    )
    top, total, acc = lax.fori_loop(0, keys.shape[0] // width, one_block, state)
    attended = (acc / total[..., None]).astype(BF16).transpose(2, 0, 1, 3).reshape(rows, -1)
    partial_out = jnp.dot(attended, w_out, preferred_element_type=F32)
    summed = lax.psum(partial_out.astype(BF16), "tp").astype(F32)
    mid = (xf + summed).astype(BF16)
    mid_f = mid.astype(F32)
    post_normed = rms(mid_f, post_gain).astype(BF16)
    gate_w = lax.all_gather(w_gate, "seq", axis=0, tiled=True)
    up_w = lax.all_gather(w_up, "seq", axis=0, tiled=True)
    down_w = lax.all_gather(w_down, "seq", axis=1, tiled=True)
    gate = jnp.dot(post_normed, gate_w, preferred_element_type=F32)
    up = jnp.dot(post_normed, up_w, preferred_element_type=F32)
    act = (jax.nn.silu(gate) * up).astype(BF16)
    terms = jnp.dot(act, down_w, preferred_element_type=F32)
    ffn_total = lax.psum(terms.astype(BF16), "tp").astype(F32)
    hidden = (mid_f + ffn_total).astype(BF16)
    return (hidden, key_cache, value_cache)


def solution(mesh):
    in_specs = (
        P("seq", None),
        P(),
        P(None, "tp"),
        P(None, "tp"),
        P(None, "tp"),
        P("tp", None),
        P(),
        P(),
        P("seq"),
        P("seq"),
        P(),
        P("seq", "tp"),
        P("seq", "tp"),
        P("tp", "seq"),
    )
    out_specs = (P("seq", None), P("seq", "tp"), P("seq", "tp"))
    body = grid_body if (mesh.shape["seq"], mesh.shape["tp"]) == (8, 4) else general_body
    return jax.shard_map(body, mesh=mesh, in_specs=in_specs, out_specs=out_specs, check_vma=False)
```
